32 devices in a mesh: attn: 2 (over z_hi), expert: 4 (over y, core), hidden: 2 (over x), pair: 2 (over z_lo).
Axes of the slice: x: 2, y: 2, z: 4 (z_hi: 2, z_lo: 2; z = z_hi * 2 + z_lo), core: 2. Of those that a mesh axis runs over, the one named last changes fastest.
Arguments:
- queries: bfloat16 [8, 128, 512], P(('expert', 'pair'), None, ('attn', 'hidden')), may hold values from -5 to 5
- keys: bfloat16 [8, 128, 256], P(('expert', 'pair'), None, 'attn'), may hold values from -5 to 5
- values: bfloat16 [8, 128, 256], P(('expert', 'pair'), None, 'attn'), may hold values from -6 to 6
- out_weight: bfloat16 [512, 4096], P(('attn', 'hidden')), may hold values from -0.25 to 0.25
- residual: bfloat16 [8, 128, 4096], P(('expert', 'pair'), ('attn', 'hidden')), may hold values from -4 to 4
- norm_gain: float32 [4096], replicated, may hold values from 0.1 to 1.9
- route_logits: float32 [8, 128, 2], P(('expert', 'pair'), ('attn', 'hidden')), may hold values from -6 to 6
- expert_ids: int32 [8, 128, 2], P(('expert', 'pair'), ('attn', 'hidden')), may hold values from 0 to 3, all different within a row; in each aligned block of 32 rows (0 to 31, 32 to 63, ..., all dimensions but the last counted through in order) at most 16 rows name the same one
- doc_lengths: int32 [8, 2], P(('expert', 'pair')), may hold values from 32 to 96, as said below
- gate_up_weight: bfloat16 [4, 2, 4096, 8192], P('expert', None, None, ('attn', 'hidden', 'pair')), may hold values from -0.09375 to 0.09375
- down_weight: bfloat16 [4, 8192, 4096], P('expert', 'attn', ('hidden', 'pair')), may hold values from -0.0625 to 0.0625
Outputs:
- layer_out: bfloat16 [8, 128, 4096], P(('expert', 'pair'), ('attn', 'hidden'))
The draws below stay inside these ranges and needn't reach their ends.
Inputs may be any that keep to these rules, and one draw needn't show every extreme that they name: `expert_ids`: A token names two different experts; in every aligned block of 32 tokens (all leading dimensions taken together, in order) no expert is named by more than 16 tokens, and in some block one expert is named by exactly 16 tokens. `doc_lengths`: each group has one document of 96 tokens and one of 32 tokens, in either order.
All inputs are finite; a program needn't handle non-finite values.
Results may differ from the reference program's by a relative error of at most 0.022.
Values may be sent and summed in bfloat16 or wider, within the bound.
A program may use at most 64 MiB of HBM per device.

```python
import math
import jax
import jax.numpy as jnp
import numpy as np
from jax import lax

D = 4096
HD = 128
FF = 8192
TOK_G = 128
H = 4
KVH = 2
EXPERTS = 4
GROUPS = 8
TOK_OWN = 32
CAP = 16
SLOTS = 512
MOST_LEN = 96


def draw_queries(key, part):
    base = jax.random.normal(jax.random.fold_in(key, 11), (GROUPS, TOK_G, H * HD), dtype=jnp.float32)
    base = jnp.clip(base, -5.0, 5.0)
    return base.astype(jnp.bfloat16)


def draw_keys(key, part):
    base = jax.random.normal(jax.random.fold_in(key, 13), (GROUPS, TOK_G, KVH * HD), dtype=jnp.float32)
    base = jnp.clip(base, -5.0, 5.0)
    return base.astype(jnp.bfloat16)


def draw_doc_lengths(key, part):
    order = jax.random.randint(jax.random.fold_in(key, 29), (GROUPS,), 0, 2, dtype=jnp.int32)
    longest = jnp.full((GROUPS,), MOST_LEN, dtype=jnp.int32)
    shortest = jnp.full((GROUPS,), TOK_G - MOST_LEN, dtype=jnp.int32)
    first = jnp.where(order > 0, longest, shortest)
    second = jnp.where(order > 0, shortest, longest)
    return jnp.stack([first, second], axis=1).astype(jnp.int32)


def levels(stream_key, shape, shards, smallest, largest):
    gain, own = 1.0, jax.random.fold_in(stream_key, 6)
    for position, shards_of in shards:
        heights = jnp.exp(jax.random.uniform(jax.random.fold_in(own, position), (shards_of,), jnp.float32, smallest / len(shards), largest / len(shards)))
        gain = gain * jnp.repeat(heights, shape[position] // shards_of).reshape([-1 if axis == position else 1 for axis in range(len(shape))])
    return gain


def routed_block(stream_key, own, number, rows, amount, top, reach, lean):
    sequence = jax.random.permutation(stream_key, amount)
    packed, ordinary = load_shares(amount, rows * top, reach, lean, True), load_shares(amount, rows * top, reach, lean, False)
    places = jnp.arange(amount)

    def named(sizes, rotation):
        used = int((sizes > 0).sum())
        fixed = max(1, used // 4)
        moved = fixed + (places - fixed + rotation * (used - fixed)) % max(1, amount - fixed)
        return jnp.zeros((amount,), jnp.int32).at[sequence[jnp.where(places < fixed, places, moved)]].set(jnp.asarray(sizes, jnp.int32))

    sizes = jnp.where(number % 4 == 0, named(packed, number // 4), named(ordinary, number - number // 4 - 1))
    mixed = jax.random.permutation(jax.random.fold_in(own, 3), amount)
    giver, sink = mixed[0:amount // 2 * 2:2], mixed[1:amount // 2 * 2:2]
    room = jnp.minimum(sizes[giver] - 1, reach - sizes[sink]) // 2
    room = jnp.where((giver == sequence[0]) | (sink == sequence[0]) | (sizes[sink] == 0), 0, jnp.maximum(room, 0))
    moved = jax.random.randint(jax.random.fold_in(own, 4), (amount // 2,), 0, 1 << 20) % (room + 1)
    sizes = sizes.at[giver].add(-moved).at[sink].add(moved)
    labels = jnp.searchsorted(jnp.cumsum(sizes), jnp.arange(rows * top), side="right").astype(jnp.int32)
    grid = labels.reshape(top, rows).T
    grid = grid[jax.random.permutation(jax.random.fold_in(own, 1), rows)]
    rotation = jax.random.randint(jax.random.fold_in(own, 2), (rows, 1), 0, top)
    return jnp.take_along_axis(grid, (jnp.arange(top)[None, :] + rotation) % top, axis=1)


def load_shares(amount, total, bound, slope, full):
    portions = [(1 << 20) // math.isqrt(rank ** slope) + 1 for rank in range(1, amount + 1)]
    largest = bound if full else min(bound, max(-(-total // amount), total * portions[0] // sum(portions)))
    least = 1 if total - largest >= amount - 1 else 0
    counts, surplus = [largest] + [least] * (amount - 1), total - largest - least * (amount - 1)
    while surplus > 0:
        movable = [i for i in range(1, amount) if counts[i] < largest] or [i for i in range(1, amount) if counts[i] < bound]
        mass, remaining = sum([portions[i] for i in movable]), surplus
        for i in movable:
            extra = min(bound - counts[i], max(1, remaining * portions[i] // mass), surplus)
            counts[i] = counts[i] + extra
            surplus = surplus - extra
    return np.array(counts)


def gaussian(own_key, dims, deviation, bound, pieces=(), kind=jnp.bfloat16):
    entries = jax.random.normal(own_key, dims, jnp.float32) * deviation
    if len(pieces) > 0:
        entries = levels(own_key, dims, pieces, -0.22, 0.18) * entries
    return jnp.clip(entries, min=-bound, max=bound).astype(kind)


def setup_inputs(seed: int = 0) -> dict:
    key_list = jax.random.split(jax.random.key(seed), 12)
    queries = draw_queries(jax.random.fold_in(key_list[11], 71), 0)
    keys = draw_keys(jax.random.fold_in(key_list[11], 71), 0)
    values = gaussian(key_list[2], (GROUPS, TOK_G, KVH * HD), 1.0, 6.0, ((0, 8), (2, 2)))
    out_weight = gaussian(key_list[3], (H * HD, D), (H * HD) ** -0.5, 0.25, ((0, 4),))
    residual = gaussian(key_list[4], (GROUPS, TOK_G, D), 0.5, 4.0, ((0, 8), (1, 4)))
    norm_gain = jnp.clip(1.0 + 0.18 * jax.random.normal(key_list[5], (D,), jnp.float32), 0.1, 1.9)
    route_logits = gaussian(key_list[6], (GROUPS, TOK_G, 2), 1.5, 6.0, ((0, 8), (1, 4)), jnp.float32)
    expert_ids_keys = jax.random.split(jax.random.fold_in(key_list[7], 1), GROUPS * TOK_G // TOK_OWN)
    expert_ids_turns = jax.random.permutation(jax.random.fold_in(key_list[7], 3), GROUPS * TOK_G // TOK_OWN)
    expert_ids = jax.vmap(lambda own, number: routed_block(jax.random.fold_in(key_list[7], 2), own, number, TOK_OWN, EXPERTS, 2, CAP, 2))(expert_ids_keys, expert_ids_turns).reshape((GROUPS, TOK_G, 2))
    doc_lengths = draw_doc_lengths(jax.random.fold_in(key_list[11], 71), 0)
    gate_up_weight = gaussian(key_list[9], (EXPERTS, 2, D, FF), D ** -0.5, 0.09375, ((0, 4), (3, 8)))
    down_weight = gaussian(key_list[10], (EXPERTS, FF, D), FF ** -0.5, 0.0625, ((0, 4), (1, 2), (2, 4)))
    return dict(queries=queries, keys=keys, values=values, out_weight=out_weight, residual=residual, norm_gain=norm_gain, route_logits=route_logits, expert_ids=expert_ids, doc_lengths=doc_lengths, gate_up_weight=gate_up_weight, down_weight=down_weight)


epsilon = 1e-05

def document_mask(lengths):
    doc_ends = jnp.cumsum(lengths)
    positions = jnp.arange(TOK_G, dtype=jnp.int32)
    document = lax.optimization_barrier(jnp.sum((positions[:, None] >= doc_ends[None, :]).astype(jnp.int32), axis=1))
    same_doc = document[:, None] == document[None, :]
    return (same_doc & (positions[None, :] <= positions[:, None])).astype(jnp.int32)

def attend_head(query_rows, key_rows, value_rows, allowed):
    scores = jnp.dot(query_rows, key_rows.T, preferred_element_type=jnp.float32) * HD ** (-0.5)
    scores = jnp.where(allowed > 0, scores, -1e+30)
    row_top = lax.optimization_barrier(jnp.max(scores, axis=1, keepdims=True))
    weights = jnp.exp(scores - row_top)
    probabilities = (weights / lax.optimization_barrier(jnp.sum(weights, axis=1, keepdims=True))).astype(jnp.bfloat16)
    return jnp.dot(probabilities, value_rows, preferred_element_type=jnp.float32).astype(jnp.bfloat16)

def reference(queries, keys, values, out_weight, residual, norm_gain, route_logits, expert_ids, doc_lengths, gate_up_weight, down_weight):

    def group_forward(inputs):
        query_group, key_group, value_group, resid_group, lengths = inputs
        allowed = document_mask(lengths)
        share = H // KVH
        query_heads = query_group.reshape(TOK_G, H, HD).transpose(1, 0, 2)
        key_heads = jnp.repeat(key_group.reshape(TOK_G, KVH, HD).transpose(1, 0, 2), share, axis=0)
        value_heads = jnp.repeat(value_group.reshape(TOK_G, KVH, HD).transpose(1, 0, 2), share, axis=0)
        heads_out = jax.vmap(attend_head, in_axes=(0, 0, 0, None))(query_heads, key_heads, value_heads, allowed)
        joined = heads_out.transpose(1, 0, 2).reshape(TOK_G, H * HD)
        attended = resid_group.astype(jnp.float32) + jnp.dot(joined, out_weight, preferred_element_type=jnp.float32)
        scale = lax.rsqrt(lax.optimization_barrier(jnp.mean(attended * attended, axis=1, keepdims=True)) + epsilon)
        normed = (attended * scale * norm_gain).astype(jnp.bfloat16)
        return (attended, normed)
    attended, normed = lax.map(group_forward, (queries, keys, values, residual, doc_lengths))
    owners = GROUPS * TOK_G // TOK_OWN
    row_total = 2 * TOK_OWN
    chosen = expert_ids.reshape(owners, row_total)
    row_ids = jnp.arange(row_total, dtype=jnp.int32)
    earlier = row_ids[None, :] < row_ids[:, None]
    same_expert = chosen[:, :, None] == chosen[:, None, :]
    ranking = lax.optimization_barrier(jnp.sum((same_expert & earlier[None]).astype(jnp.int32), axis=2))
    owner_ids = jnp.arange(owners, dtype=jnp.int32)
    slot_of_row = (chosen * SLOTS + owner_ids[:, None] * CAP + ranking).reshape(-1)
    token_of_row = (owner_ids[:, None] * TOK_OWN + row_ids[None, :] // 2).reshape(-1)
    slot_token = jnp.zeros((EXPERTS * SLOTS,), jnp.int32).at[slot_of_row].set(token_of_row)
    slot_filled = jnp.zeros((EXPERTS * SLOTS,), jnp.int32).at[slot_of_row].set(1)
    flat_normed = normed.reshape(GROUPS * TOK_G, D)
    picked = jnp.take(flat_normed, slot_token, axis=0)
    picked = jnp.where(slot_filled[:, None] > 0, picked, jnp.zeros_like(picked))
    expert_rows = picked.reshape(EXPERTS, SLOTS, D)

    def expert_forward(inputs):
        rows, gate_up, down = inputs
        gate = jnp.dot(rows, gate_up[0], preferred_element_type=jnp.float32)
        upward = jnp.dot(rows, gate_up[1], preferred_element_type=jnp.float32)
        activated = (jax.nn.silu(gate) * upward).astype(jnp.bfloat16)
        return jnp.dot(activated, down, preferred_element_type=jnp.float32).astype(jnp.bfloat16)
    expert_out = lax.map(expert_forward, (expert_rows, gate_up_weight, down_weight)).reshape(EXPERTS * SLOTS, D)
    row_out = jnp.take(expert_out, slot_of_row, axis=0).reshape(GROUPS, TOK_G, 2, D).astype(jnp.float32)
    first_share = jax.nn.sigmoid(route_logits[..., 0] - route_logits[..., 1])
    layer_out = attended + first_share[..., None] * row_out[:, :, 0] + (1.0 - first_share)[..., None] * row_out[:, :, 1]
    return layer_out.astype(jnp.bfloat16)
```

```python
import jax
import jax.numpy as jnp
from jax import lax
from jax.sharding import PartitionSpec as P

D = 4096
HD = 128


epsilon = 1e-05


def rank_rows(chosen):
    row_total = chosen.shape[-1]
    row_ids = jnp.arange(row_total, dtype=jnp.int32)
    earlier = row_ids[None, :] < row_ids[:, None]
    same_expert = chosen[..., :, None] == chosen[..., None, :]
    return jnp.sum((same_expert & earlier).astype(jnp.int32), axis=-1)


def body(
    queries,
    keys,
    values,
    out_weight,
    residual,
    norm_gain,
    route_logits,
    expert_ids,
    doc_lengths,
    gate_up_weight,
    down_weight,
):
    tok_group = queries.shape[1]
    lengths = doc_lengths[0]
    order = jnp.arange(lengths.shape[0], dtype=jnp.int32)
    doc_ends = jnp.sum(jnp.where(order[None, :] <= order[:, None], lengths[None, :], 0), axis=1)
    positions = jnp.arange(tok_group, dtype=jnp.int32)
    document = jnp.sum((positions[:, None] >= doc_ends[None, :]).astype(jnp.int32), axis=1)
    allowed = (document[:, None] == document[None, :]) & (positions[None, :] <= positions[:, None])
    scores = jnp.dot(queries[0], keys[0].T, preferred_element_type=jnp.float32) * HD ** (-0.5)
    scores = jnp.where(allowed, scores, -1e30)
    row_top = jnp.max(scores, axis=1, keepdims=True)
    weights = jnp.exp(scores - row_top)
    probabilities = (weights / jnp.sum(weights, axis=1, keepdims=True)).astype(jnp.bfloat16)
    heads_out = jnp.dot(probabilities, values[0], preferred_element_type=jnp.float32).astype(
        jnp.bfloat16
    )
    owned_rows = tok_group // lax.axis_size(("attn", "hidden"))
    subset = heads_out
    owned = lax.psum_scatter(
        jnp.dot(subset, out_weight, preferred_element_type=jnp.float32).astype(jnp.bfloat16),
        ("attn", "hidden"),
        scatter_dimension=0,
        tiled=True,
    ).astype(jnp.float32)
    attended = residual[0].astype(jnp.float32) + owned
    scale = lax.rsqrt(jnp.mean(attended * attended, axis=1, keepdims=True) + epsilon)
    normed = (attended * scale * norm_gain).astype(jnp.bfloat16)
    expert_count = lax.axis_size("expert")
    row_total = 2 * owned_rows
    capacity = max(2, (row_total + expert_count - 1) // expert_count)
    chosen = expert_ids[0].reshape(row_total)
    ranking = rank_rows(chosen)
    targets = jnp.arange(expert_count * capacity, dtype=jnp.int32)
    expert_of_slot = targets // capacity
    rank_of_slot = targets % capacity
    selector = (
        (chosen[None, :] == expert_of_slot[:, None]) & (ranking[None, :] == rank_of_slot[:, None])
    ).astype(jnp.bfloat16)
    repeated = jnp.repeat(normed, 2, axis=0)
    outgoing = jnp.dot(selector, repeated, preferred_element_type=jnp.float32).astype(jnp.bfloat16)
    outgoing = outgoing.reshape(expert_count, capacity, D)
    arrived = lax.all_to_all(outgoing, "expert", split_axis=0, concat_axis=0, tiled=True).reshape(
        expert_count * capacity, D
    )
    gate_up = jnp.einsum(
        "rd,gdf->rgf",
        lax.all_gather(arrived, ("attn", "hidden", "pair"), axis=0, tiled=True),
        gate_up_weight[0],
        preferred_element_type=jnp.float32,
    )
    activated = (jax.nn.silu(gate_up[:, 0]) * gate_up[:, 1]).astype(jnp.bfloat16)
    block_units = lax.all_gather(activated, ("hidden", "pair"), axis=1, tiled=True)
    down_local = down_weight[0]
    subset = block_units
    expert_out = lax.psum_scatter(
        jnp.dot(subset, down_local, preferred_element_type=jnp.float32).astype(jnp.bfloat16),
        "attn",
        scatter_dimension=0,
        tiled=True,
    )
    column_width = expert_out.shape[1]
    pair_count = lax.axis_size(("hidden", "pair"))
    tile_grid = expert_out.reshape(pair_count, expert_count, capacity, column_width)
    outgoing_wide = tile_grid.transpose(1, 0, 2, 3).reshape(
        expert_count * pair_count, 1, capacity, column_width
    )
    returned = lax.all_to_all(
        outgoing_wide, ("expert", "hidden", "pair"), split_axis=0, concat_axis=1, tiled=True
    )
    returned = returned.reshape(expert_count, pair_count, capacity, column_width).transpose(
        0, 2, 1, 3
    )
    returned = returned.reshape(expert_count * capacity, D)
    per_row = jnp.einsum(
        "sr,sd->rd", selector, returned, preferred_element_type=jnp.float32
    ).reshape(owned_rows, 2, D)
    logits = route_logits[0]
    first_share = jax.nn.sigmoid(logits[:, 0] - logits[:, 1])
    layer_out = (
        attended
        + first_share[:, None] * per_row[:, 0]
        + (1.0 - first_share)[:, None] * per_row[:, 1]
    )
    return layer_out.astype(jnp.bfloat16)[None]


def solution(mesh):
    in_specs = (
        P(("expert", "pair"), None, ("attn", "hidden")),
        P(("expert", "pair"), None, "attn"),
        P(("expert", "pair"), None, "attn"),
        P(("attn", "hidden"), None),
        P(("expert", "pair"), ("attn", "hidden"), None),
        P(),
        P(("expert", "pair"), ("attn", "hidden"), None),
        P(("expert", "pair"), ("attn", "hidden"), None),
        P(("expert", "pair"), None),
        P("expert", None, None, ("attn", "hidden", "pair")),
        P("expert", "attn", ("hidden", "pair")),
    )
    out_specs = P(("expert", "pair"), ("attn", "hidden"), None)
    return jax.shard_map(body, mesh=mesh, in_specs=in_specs, out_specs=out_specs, check_vma=False)
```

```python
import functools

import jax
import jax.numpy as jnp
from jax import lax
from jax.experimental import pallas as pl
from jax.experimental.pallas import tpu as pltpu
from jax.sharding import PartitionSpec as P

D = 4096
HD = 128


epsilon = 1e-05


def rank_rows(chosen):
    row_total = chosen.shape[-1]
    row_ids = jnp.arange(row_total, dtype=jnp.int32)
    earlier = row_ids[None, :] < row_ids[:, None]
    same_expert = chosen[..., :, None] == chosen[..., None, :]
    return jnp.sum((same_expert & earlier).astype(jnp.int32), axis=-1)


def attention(queries, keys, values, doc_lengths):
    tok_group = queries.shape[1]
    lengths = doc_lengths[0]
    order = jnp.arange(lengths.shape[0], dtype=jnp.int32)
    doc_ends = jnp.sum(jnp.where(order[None, :] <= order[:, None], lengths[None, :], 0), axis=1)
    positions = jnp.arange(tok_group, dtype=jnp.int32)
    document = jnp.sum((positions[:, None] >= doc_ends[None, :]).astype(jnp.int32), axis=1)
    allowed = (document[:, None] == document[None, :]) & (positions[None, :] <= positions[:, None])
    scores = jnp.dot(queries[0], keys[0].T, preferred_element_type=jnp.float32) * HD ** (-0.5)
    scores = jnp.where(allowed, scores, -1e30)
    row_top = jnp.max(scores, axis=1, keepdims=True)
    weights = jnp.exp(scores - row_top)
    probabilities = (weights / jnp.sum(weights, axis=1, keepdims=True)).astype(jnp.bfloat16)
    heads_out = jnp.dot(probabilities, values[0], preferred_element_type=jnp.float32).astype(
        jnp.bfloat16
    )
    return heads_out


def plain_body(
    queries,
    keys,
    values,
    out_weight,
    residual,
    norm_gain,
    route_logits,
    expert_ids,
    doc_lengths,
    gate_up_weight,
    down_weight,
):
    tok_group = queries.shape[1]
    heads_out = attention(queries, keys, values, doc_lengths)
    owned_rows = tok_group // lax.axis_size(("attn", "hidden"))
    subset = heads_out
    owned = lax.psum_scatter(
        jnp.dot(subset, out_weight, preferred_element_type=jnp.float32).astype(jnp.bfloat16),
        ("attn", "hidden"),
        scatter_dimension=0,
        tiled=True,
    ).astype(jnp.float32)
    attended = residual[0].astype(jnp.float32) + owned
    scale = lax.rsqrt(jnp.mean(attended * attended, axis=1, keepdims=True) + epsilon)
    normed = (attended * scale * norm_gain).astype(jnp.bfloat16)
    expert_count = lax.axis_size("expert")
    row_total = 2 * owned_rows
    capacity = max(2, (row_total + expert_count - 1) // expert_count)
    chosen = expert_ids[0].reshape(row_total)
    ranking = rank_rows(chosen)
    targets = jnp.arange(expert_count * capacity, dtype=jnp.int32)
    expert_of_slot = targets // capacity
    rank_of_slot = targets % capacity
    selector = (
        (chosen[None, :] == expert_of_slot[:, None]) & (ranking[None, :] == rank_of_slot[:, None])
    ).astype(jnp.bfloat16)
    repeated = jnp.repeat(normed, 2, axis=0)
    outgoing = jnp.dot(selector, repeated, preferred_element_type=jnp.float32).astype(jnp.bfloat16)
    outgoing = outgoing.reshape(expert_count, capacity, D)
    arrived = lax.all_to_all(outgoing, "expert", split_axis=0, concat_axis=0, tiled=True).reshape(
        expert_count * capacity, D
    )
    gate_up = jnp.einsum(
        "rd,gdf->rgf",
        lax.all_gather(arrived, ("attn", "hidden", "pair"), axis=0, tiled=True),
        gate_up_weight[0],
        preferred_element_type=jnp.float32,
    )
    activated = (jax.nn.silu(gate_up[:, 0]) * gate_up[:, 1]).astype(jnp.bfloat16)
    block_units = lax.all_gather(activated, ("hidden", "pair"), axis=1, tiled=True)
    down_local = down_weight[0]
    subset = block_units
    expert_out = lax.psum_scatter(
        jnp.dot(subset, down_local, preferred_element_type=jnp.float32).astype(jnp.bfloat16),
        "attn",
        scatter_dimension=0,
        tiled=True,
    )
    column_width = expert_out.shape[1]
    pair_count = lax.axis_size(("hidden", "pair"))
    tile_grid = expert_out.reshape(pair_count, expert_count, capacity, column_width)
    outgoing_wide = tile_grid.transpose(1, 0, 2, 3).reshape(
        expert_count * pair_count, 1, capacity, column_width
    )
    returned = lax.all_to_all(
        outgoing_wide, ("expert", "hidden", "pair"), split_axis=0, concat_axis=1, tiled=True
    )
    returned = returned.reshape(expert_count, pair_count, capacity, column_width).transpose(
        0, 2, 1, 3
    )
    returned = returned.reshape(expert_count * capacity, D)
    per_row = jnp.einsum(
        "sr,sd->rd", selector, returned, preferred_element_type=jnp.float32
    ).reshape(owned_rows, 2, D)
    logits = route_logits[0]
    first_share = jax.nn.sigmoid(logits[:, 0] - logits[:, 1])
    layer_out = (
        attended
        + first_share[:, None] * per_row[:, 0]
        + (1.0 - first_share)[:, None] * per_row[:, 1]
    )
    return layer_out.astype(jnp.bfloat16)[None]


def layer_kernel(
    sizes,
    heads_ref,
    out_weight_ref,
    residual_ref,
    gain_ref,
    pick_ref,
    back_ref,
    share_ref,
    gate_up_hbm,
    down_hbm,
    out_ref,
    gate_up_ref,
    down_ref,
    part_ref,
    sums_ref,
    attended_ref,
    outgoing_ref,
    rows_ref,
    acts_ref,
    stage_ref,
    returned_ref,
    weight_sem,
    send_sem,
    recv_sem,
):
    n_attn, n_expert, n_hidden, n_pair, own, cap = sizes
    names = ("attn", "expert", "hidden", "pair")
    counts = (n_attn, n_expert, n_hidden, n_pair)
    me = tuple(lax.axis_index(name) for name in names)
    a, e, h, p = me
    width = rows_ref.shape[1]
    units = acts_ref.shape[2]
    columns = down_ref.shape[1]
    block = n_expert * cap
    chunk = n_hidden * block
    chunks = n_attn * n_pair
    half = chunk // 2
    pending = []

    def shifted(offset, sign=1):
        return tuple(
            lax.rem(x + (sign * d) % n, n) if d else x for x, d, n in zip(me, offset, counts)
        )

    def copy(src, dst, sem, target):
        return pltpu.make_async_remote_copy(
            src_ref=src,
            dst_ref=dst,
            send_sem=send_sem.at[sem],
            recv_sem=recv_sem.at[sem],
            device_id=dict(zip(names, target)),
            device_id_type=pl.DeviceIdType.MESH,
        )

    def send(src, dst, sem, target):
        started = copy(src, dst, sem, target)
        started.start()
        pending.append(started)

    def arrive(ref, sem):
        copy(ref, ref, sem, shifted((0, 1, 0, 0))).wait_recv()

    def at(start, size, align=16):
        return pl.ds(pl.multiple_of(start, align), size)

    weights = [
        pltpu.make_async_copy(gate_up_hbm.at[0], gate_up_ref, weight_sem.at[0]),
        pltpu.make_async_copy(down_hbm.at[0], down_ref, weight_sem.at[1]),
    ]
    for load in weights:
        load.start()

    barrier = pltpu.get_barrier_semaphore()
    others = [
        (da, de, dh, dp)
        for da in range(n_attn)
        for de in range(n_expert)
        for dh in range(n_hidden)
        for dp in range(n_pair)
        if (da, de, dh, dp) != (0, 0, 0, 0)
    ]
    for offset in others:
        pl.semaphore_signal(
            barrier,
            inc=1,
            device_id=dict(zip(names, shifted(offset))),
            device_id_type=pl.DeviceIdType.MESH,
        )
    pl.semaphore_wait(barrier, len(others))

    used = 0

    def numbers(count):
        nonlocal used
        used += count
        return used - count

    first = numbers(n_attn * n_hidden)
    mine = a * n_hidden + h
    for da in reversed(range(n_attn)):
        for dh in reversed(range(n_hidden)):
            target = shifted((da, 0, dh, 0))
            owner = target[0] * n_hidden + target[2]
            partial = jnp.dot(
                heads_ref[at(owner * own, own), :],
                out_weight_ref[...],
                preferred_element_type=jnp.float32,
            )
            if da or dh:
                slot = da * n_hidden + dh
                part_ref[slot] = partial.astype(jnp.bfloat16)
                send(part_ref.at[slot], sums_ref.at[mine], first + slot, target)
            else:
                attended_ref[...] = partial + residual_ref[0].astype(jnp.float32)
    for da in range(n_attn):
        for dh in range(n_hidden):
            if da or dh:
                source = shifted((da, 0, dh, 0), -1)
                slot = source[0] * n_hidden + source[2]
                arrive(sums_ref.at[slot], first + da * n_hidden + dh)
                attended_ref[...] += sums_ref[slot].astype(jnp.float32)
    attended = attended_ref[...]
    scale = lax.rsqrt(jnp.mean(attended * attended, axis=1, keepdims=True) + epsilon)
    normed = (attended * scale * gain_ref[...]).astype(jnp.bfloat16)
    outgoing_ref[...] = jnp.dot(
        pick_ref[...], normed, preferred_element_type=jnp.float32
    ).astype(jnp.bfloat16)

    base = ((a * n_pair + p) * n_hidden + h) * block
    first = numbers(n_expert)
    for de in reversed(range(1, n_expert)):
        target = shifted((0, de, 0, 0))
        send(
            outgoing_ref.at[at(target[1] * cap, cap)],
            rows_ref.at[at(base + e * cap, cap)],
            first + de,
            target,
        )
    rows_ref[at(base + e * cap, cap), :] = outgoing_ref[at(e * cap, cap), :]
    for de in range(1, n_expert):
        source = shifted((0, de, 0, 0), -1)
        arrive(rows_ref.at[at(base + source[1] * cap, cap)], first + de)

    steps = [(da, dp) for da in range(n_attn) for dp in range(n_pair)]
    along = numbers(chunks)
    across = numbers(chunks * n_hidden)

    def spread(step, start):
        for dh in range(1, n_hidden):
            block_ref = rows_ref.at[at(start, block)]
            send(block_ref, block_ref, across + step * n_hidden + dh, shifted((0, 0, dh, 0)))

    own_rows = rows_ref.at[at(base, block)]
    spread(0, base)
    for step, (da, dp) in enumerate(steps):
        if step:
            send(own_rows, own_rows, along + step, shifted((da, 0, 0, dp)))

    def chunk_of(step):
        da, dp = steps[step]
        source = shifted((da, 0, 0, dp), -1)
        return source[0] * n_pair + source[3]

    def forward(step):
        start = (chunk_of(step) * n_hidden + h) * block
        arrive(rows_ref.at[at(start, block)], along + step)
        spread(step, start)

    near = numbers(chunks * n_hidden * 2)
    side = numbers(chunks * n_pair * 2)
    turn_side = numbers(chunks * n_hidden * n_pair)
    turn_near = numbers(chunks * n_hidden * n_pair)
    group = h * n_pair + p

    def piece(owner, c, part):
        return acts_ref.at[owner, at(c * chunk + part * half, half)]

    def up(step):
        c = chunk_of(step)
        for dh in range(1, n_hidden):
            source = shifted((0, 0, dh, 0), -1)
            start = (c * n_hidden + source[2]) * block
            arrive(rows_ref.at[at(start, block)], across + step * n_hidden + dh)
        tile = min(256, units)

        @pl.loop(0, units // tile)
        def _(t):
            where = at(t * tile, tile, 128)
            rows = rows_ref[at(c * chunk, chunk), :]
            gate = jnp.dot(rows, gate_up_ref[0, :, where], preferred_element_type=jnp.float32)
            upward = jnp.dot(rows, gate_up_ref[1, :, where], preferred_element_type=jnp.float32)
            acts_ref[group, at(c * chunk, chunk), where] = (
                gate / (1.0 + jnp.exp(-gate)) * upward
            ).astype(jnp.bfloat16)

        for part in range(2):
            mine_ref = piece(group, c, part)
            for dh in range(1, n_hidden):
                sem = near + (c * n_hidden + dh) * 2 + part
                send(mine_ref, mine_ref, sem, shifted((0, 0, dh, 0)))
            for dp in range(1, n_pair):
                sem = side + (c * n_pair + dp) * 2 + part
                send(mine_ref, mine_ref, sem, shifted((0, 0, 0, dp)))

    def turn(step):
        c = chunk_of(step)
        for dh in range(1, n_hidden):
            owner = shifted((0, 0, dh, 0), -1)[2] * n_pair + p
            landed = piece(owner, c, 0)
            arrive(landed, near + (c * n_hidden + dh) * 2)
            for dp in range(1, n_pair):
                sem = turn_side + (c * n_hidden + dh) * n_pair + dp
                send(landed, landed, sem, shifted((0, 0, 0, dp)))
        for dp in range(1, n_pair):
            owner = h * n_pair + shifted((0, 0, 0, dp), -1)[3]
            landed = piece(owner, c, 1)
            arrive(landed, side + (c * n_pair + dp) * 2 + 1)
            for dh in range(1, n_hidden):
                sem = turn_near + (c * n_hidden + dh) * n_pair + dp
                send(landed, landed, sem, shifted((0, 0, dh, 0)))

    last = numbers(n_attn * n_expert * n_hidden * n_pair)

    def number(da, de, dh, dp):
        return last + ((da * n_expert + de) * n_hidden + dh) * n_pair + dp

    def down(step):
        c = chunk_of(step)
        for dh in range(1, n_hidden):
            owner = shifted((0, 0, dh, 0), -1)[2] * n_pair + p
            arrive(piece(owner, c, 1), near + (c * n_hidden + dh) * 2 + 1)
        for dp in range(1, n_pair):
            owner = h * n_pair + shifted((0, 0, 0, dp), -1)[3]
            arrive(piece(owner, c, 0), side + (c * n_pair + dp) * 2)
        for dh in range(1, n_hidden):
            for dp in range(1, n_pair):
                source = shifted((0, 0, dh, dp), -1)
                owner = source[2] * n_pair + source[3]
                sem = (c * n_hidden + dh) * n_pair + dp
                arrive(piece(owner, c, 0), turn_side + sem)
                arrive(piece(owner, c, 1), turn_near + sem)
        tile = min(256, columns)

        @pl.loop(0, columns // tile)
        def _(t):
            where = at(t * tile, tile, 128)
            total = jnp.zeros((chunk, tile), jnp.float32)
            for k in range(n_hidden * n_pair):
                total += jnp.dot(
                    acts_ref[k, at(c * chunk, chunk), :],
                    down_ref[k * units : (k + 1) * units, where],
                    preferred_element_type=jnp.float32,
                )
            stage_ref[at(c * chunk, chunk), where] = total.astype(jnp.bfloat16)

        da, dp = steps[step]
        for dh in range(n_hidden):
            for de in range(n_expert):
                offset = ((-da) % n_attn, de, dh, (-dp) % n_pair)
                target = shifted(offset)
                start = (c * n_hidden + target[2]) * block + target[1] * cap
                landing = (a, group, at(e * cap, cap))
                if any(offset):
                    send(
                        stage_ref.at[at(start, cap)],
                        returned_ref.at[landing],
                        number(*offset),
                        target,
                    )
                else:
                    returned_ref[landing] = stage_ref[at(start, cap), :]

    weights[0].wait()
    total_steps = len(steps)
    if total_steps > 1:
        forward(1)
    for step in range(total_steps):
        up(step)
        if step + 2 < total_steps:
            forward(step + 2)
        if step == 0:
            weights[1].wait()
        if step % n_pair == n_pair - 1 and step >= 2 * n_pair - 1:
            for earlier in range(step - 2 * n_pair + 1, step - n_pair + 1):
                turn(earlier)
    for step in range(max(0, total_steps - n_pair), total_steps):
        turn(step)
    for step in range(total_steps):
        down(step)

    for offset in others:
        source = shifted(offset, -1)
        arrive(
            returned_ref.at[
                source[0], source[2] * n_pair + source[3], at(source[1] * cap, cap)
            ],
            number(*offset),
        )
    for k in range(n_hidden * n_pair):
        where = slice(k * columns, (k + 1) * columns)
        total = returned_ref[0, k].astype(jnp.float32)
        for other in range(1, n_attn):
            total += returned_ref[other, k].astype(jnp.float32)
        rows = total.astype(jnp.bfloat16)
        sums = attended_ref[:, where]
        for choice in range(2):
            sums += share_ref[choice] * jnp.dot(
                back_ref[choice], rows, preferred_element_type=jnp.float32
            )
        out_ref[0, :, where] = sums.astype(jnp.bfloat16)
    for started in pending:
        started.wait_send()


def fused_body(
    mesh,
    queries,
    keys,
    values,
    out_weight,
    residual,
    norm_gain,
    route_logits,
    expert_ids,
    doc_lengths,
    gate_up_weight,
    down_weight,
):
    heads_out = attention(queries, keys, values, doc_lengths)
    n_attn, n_expert, n_hidden, n_pair = (
        mesh.shape[name] for name in ("attn", "expert", "hidden", "pair")
    )
    own, width = residual.shape[1:]
    units, columns = gate_up_weight.shape[3], down_weight.shape[2]
    cap = capacity_of(own, n_expert)
    block = n_expert * cap
    groups = n_hidden * n_pair
    slots = n_attn * groups * block
    chosen = expert_ids[0].reshape(2 * own)
    slot_of_row = chosen * cap + rank_rows(chosen)
    slots_of = slot_of_row.reshape(own, 2)
    slot_ids = jnp.arange(block, dtype=jnp.int32)
    back = (slots_of.T[:, :, None] == slot_ids[None, None, :]).astype(jnp.bfloat16)
    pick = jnp.any(slots_of[None] == slot_ids[:, None, None], axis=2).astype(jnp.bfloat16)
    logits = route_logits[0]
    first_share = jax.nn.sigmoid(logits[:, 0] - logits[:, 1])
    shares = jnp.stack([first_share, 1.0 - first_share])[:, :, None]
    vmem = pl.BlockSpec(memory_space=pltpu.VMEM)
    hbm = pl.BlockSpec(memory_space=pl.ANY)
    flops = 2 * slots * (width * 2 * units + groups * units * columns)
    return pl.pallas_call(
        functools.partial(layer_kernel, (n_attn, n_expert, n_hidden, n_pair, own, cap)),
        out_shape=jax.ShapeDtypeStruct(residual.shape, jnp.bfloat16),
        in_specs=[vmem] * 7 + [hbm] * 2,
        out_specs=vmem,
        scratch_shapes=[
            pltpu.VMEM(gate_up_weight.shape[1:], jnp.bfloat16),
            pltpu.VMEM(down_weight.shape[1:], jnp.bfloat16),
            pltpu.VMEM((n_attn * n_hidden, own, width), jnp.bfloat16),
            pltpu.VMEM((n_attn * n_hidden, own, width), jnp.bfloat16),
            pltpu.VMEM((own, width), jnp.float32),
            pltpu.VMEM((block, width), jnp.bfloat16),
            pltpu.VMEM((slots, width), jnp.bfloat16),
            pltpu.VMEM((groups, slots, units), jnp.bfloat16),
            pltpu.VMEM((slots, columns), jnp.bfloat16),
            pltpu.VMEM((n_attn, groups, block, columns), jnp.bfloat16),
            pltpu.SemaphoreType.DMA((2,)),
            pltpu.SemaphoreType.DMA((semaphores(n_attn, n_expert, n_hidden, n_pair),)),
            pltpu.SemaphoreType.DMA((semaphores(n_attn, n_expert, n_hidden, n_pair),)),
        ],
        compiler_params=pltpu.CompilerParams(
            collective_id=0, has_side_effects=True, vmem_limit_bytes=58 * 2**20
        ),
        cost_estimate=pl.CostEstimate(
            flops=flops,
            bytes_accessed=2 * (gate_up_weight.size + down_weight.size),
            transcendentals=slots * units,
        ),
    )(
        heads_out,
        out_weight,
        residual,
        norm_gain[None],
        pick,
        back,
        shares,
        gate_up_weight,
        down_weight,
    )


def semaphores(n_attn, n_expert, n_hidden, n_pair):
    chunks = n_attn * n_pair
    return (
        n_attn * n_hidden
        + n_expert
        + chunks
        + chunks * n_hidden
        + 2 * chunks * n_hidden
        + 2 * chunks * n_pair
        + 2 * chunks * n_hidden * n_pair
        + n_attn * n_expert * n_hidden * n_pair
    )


def capacity_of(own, n_expert):
    return max(2, (2 * own + n_expert - 1) // n_expert)


def body_of(mesh, *arrays):
    own = arrays[4].shape[1]
    cap = capacity_of(own, mesh.shape["expert"])
    whole_tiles = own % 16 == 0 and cap % 16 == 0
    if whole_tiles:
        return fused_body(mesh, *arrays)
    return plain_body(*arrays)


def solution(mesh):
    in_specs = (
        P(("expert", "pair"), None, ("attn", "hidden")),
        P(("expert", "pair"), None, "attn"),
        P(("expert", "pair"), None, "attn"),
        P(("attn", "hidden"), None),
        P(("expert", "pair"), ("attn", "hidden"), None),
        P(),
        P(("expert", "pair"), ("attn", "hidden"), None),
        P(("expert", "pair"), ("attn", "hidden"), None),
        P(("expert", "pair"), None),
        P("expert", None, None, ("attn", "hidden", "pair")),
        P("expert", "attn", ("hidden", "pair")),
    )
    out_specs = P(("expert", "pair"), ("attn", "hidden"), None)
    body = functools.partial(body_of, mesh)
    return jax.shard_map(body, mesh=mesh, in_specs=in_specs, out_specs=out_specs, check_vma=False)
```

```python
import functools

import jax
import jax.numpy as jnp
from jax import lax
from jax.experimental import pallas as pl
from jax.experimental.pallas import tpu as pltpu
from jax.sharding import PartitionSpec as P

D = 4096
HD = 128


epsilon = 1e-05


def rank_rows(chosen):
    row_total = chosen.shape[-1]
    row_ids = jnp.arange(row_total, dtype=jnp.int32)
    earlier = row_ids[None, :] < row_ids[:, None]
    same_expert = chosen[..., :, None] == chosen[..., None, :]
    return jnp.sum((same_expert & earlier).astype(jnp.int32), axis=-1)


def attention(queries, keys, values, doc_lengths):
    tok_group = queries.shape[1]
    lengths = doc_lengths[0]
    order = jnp.arange(lengths.shape[0], dtype=jnp.int32)
    doc_ends = jnp.sum(jnp.where(order[None, :] <= order[:, None], lengths[None, :], 0), axis=1)
    positions = jnp.arange(tok_group, dtype=jnp.int32)
    document = jnp.sum((positions[:, None] >= doc_ends[None, :]).astype(jnp.int32), axis=1)
    allowed = (document[:, None] == document[None, :]) & (positions[None, :] <= positions[:, None])
    scores = jnp.dot(queries[0], keys[0].T, preferred_element_type=jnp.float32) * HD ** (-0.5)
    scores = jnp.where(allowed, scores, -1e30)
    row_top = jnp.max(scores, axis=1, keepdims=True)
    weights = jnp.exp(scores - row_top)
    probabilities = (weights / jnp.sum(weights, axis=1, keepdims=True)).astype(jnp.bfloat16)
    heads_out = jnp.dot(probabilities, values[0], preferred_element_type=jnp.float32).astype(
        jnp.bfloat16
    )
    return heads_out


def plain_body(
    queries,
    keys,
    values,
    out_weight,
    residual,
    norm_gain,
    route_logits,
    expert_ids,
    doc_lengths,
    gate_up_weight,
    down_weight,
):
    tok_group = queries.shape[1]
    heads_out = attention(queries, keys, values, doc_lengths)
    owned_rows = tok_group // lax.axis_size(("attn", "hidden"))
    subset = heads_out
    owned = lax.psum_scatter(
        jnp.dot(subset, out_weight, preferred_element_type=jnp.float32).astype(jnp.bfloat16),
        ("attn", "hidden"),
        scatter_dimension=0,
        tiled=True,
    ).astype(jnp.float32)
    attended = residual[0].astype(jnp.float32) + owned
    scale = lax.rsqrt(jnp.mean(attended * attended, axis=1, keepdims=True) + epsilon)
    normed = (attended * scale * norm_gain).astype(jnp.bfloat16)
    expert_count = lax.axis_size("expert")
    row_total = 2 * owned_rows
    capacity = max(2, (row_total + expert_count - 1) // expert_count)
    chosen = expert_ids[0].reshape(row_total)
    ranking = rank_rows(chosen)
    targets = jnp.arange(expert_count * capacity, dtype=jnp.int32)
    expert_of_slot = targets // capacity
    rank_of_slot = targets % capacity
    selector = (
        (chosen[None, :] == expert_of_slot[:, None]) & (ranking[None, :] == rank_of_slot[:, None])
    ).astype(jnp.bfloat16)
    repeated = jnp.repeat(normed, 2, axis=0)
    outgoing = jnp.dot(selector, repeated, preferred_element_type=jnp.float32).astype(jnp.bfloat16)
    outgoing = outgoing.reshape(expert_count, capacity, D)
    arrived = lax.all_to_all(outgoing, "expert", split_axis=0, concat_axis=0, tiled=True).reshape(
        expert_count * capacity, D
    )
    gate_up = jnp.einsum(
        "rd,gdf->rgf",
        lax.all_gather(arrived, ("attn", "hidden", "pair"), axis=0, tiled=True),
        gate_up_weight[0],
        preferred_element_type=jnp.float32,
    )
    activated = (jax.nn.silu(gate_up[:, 0]) * gate_up[:, 1]).astype(jnp.bfloat16)
    block_units = lax.all_gather(activated, ("hidden", "pair"), axis=1, tiled=True)
    down_local = down_weight[0]
    subset = block_units
    expert_out = lax.psum_scatter(
        jnp.dot(subset, down_local, preferred_element_type=jnp.float32).astype(jnp.bfloat16),
        "attn",
        scatter_dimension=0,
        tiled=True,
    )
    column_width = expert_out.shape[1]
    pair_count = lax.axis_size(("hidden", "pair"))
    tile_grid = expert_out.reshape(pair_count, expert_count, capacity, column_width)
    outgoing_wide = tile_grid.transpose(1, 0, 2, 3).reshape(
        expert_count * pair_count, 1, capacity, column_width
    )
    returned = lax.all_to_all(
        outgoing_wide, ("expert", "hidden", "pair"), split_axis=0, concat_axis=1, tiled=True
    )
    returned = returned.reshape(expert_count, pair_count, capacity, column_width).transpose(
        0, 2, 1, 3
    )
    returned = returned.reshape(expert_count * capacity, D)
    per_row = jnp.einsum(
        "sr,sd->rd", selector, returned, preferred_element_type=jnp.float32
    ).reshape(owned_rows, 2, D)
    logits = route_logits[0]
    first_share = jax.nn.sigmoid(logits[:, 0] - logits[:, 1])
    layer_out = (
        attended
        + first_share[:, None] * per_row[:, 0]
        + (1.0 - first_share)[:, None] * per_row[:, 1]
    )
    return layer_out.astype(jnp.bfloat16)[None]


def attend(queries, keys, values, lengths_ref):
    tok_group = queries.shape[0]
    places = (tok_group, tok_group)
    row, column = (lax.broadcasted_iota(jnp.int32, places, axis) for axis in range(2))
    row_document, column_document = jnp.zeros(places, jnp.int32), jnp.zeros(places, jnp.int32)
    end = 0
    for document in range(lengths_ref.shape[1]):
        end = end + lengths_ref[0, document]
        row_document += (row >= end).astype(jnp.int32)
        column_document += (column >= end).astype(jnp.int32)
    allowed = (row_document == column_document) & (column <= row)
    scores = lax.dot_general(
        queries, keys, (((1,), (1,)), ((), ())), preferred_element_type=jnp.float32
    ) * HD ** (-0.5)
    scores = jnp.where(allowed, scores, -1e30)
    weights = jnp.exp(scores - jnp.max(scores, axis=1, keepdims=True))
    probabilities = (weights / jnp.sum(weights, axis=1, keepdims=True)).astype(jnp.bfloat16)
    return jnp.dot(probabilities, values, preferred_element_type=jnp.float32).astype(
        jnp.bfloat16
    )


def routing(ids_ref, logits_ref, n_expert, cap):
    own = ids_ref.shape[2]
    block = n_expert * cap
    ids = [ids_ref[0, choice : choice + 1, :] for choice in range(2)]
    experts = lax.broadcasted_iota(jnp.int32, (max(8, n_expert), own), 0)
    named = [(experts == row).astype(jnp.float32) for row in ids]
    row, column = (lax.broadcasted_iota(jnp.int32, (own, own), axis) for axis in range(2))
    earlier = (row < column).astype(jnp.bfloat16)
    before = jnp.dot(
        (named[0] + named[1]).astype(jnp.bfloat16), earlier, preferred_element_type=jnp.float32
    )
    slots = [
        one * float(cap) + jnp.sum(before * which, axis=0, keepdims=True)
        for one, which in zip([one.astype(jnp.float32) for one in ids], named)
    ]

    def upright(values):
        return jnp.sum(jnp.where(row == column, values, 0.0), axis=1, keepdims=True)

    down_slots = lax.broadcasted_iota(jnp.int32, (block, own), 0).astype(jnp.float32)
    across_slots = lax.broadcasted_iota(jnp.int32, (own, block), 1).astype(jnp.float32)
    pick = sum((down_slots == slot).astype(jnp.float32) for slot in slots).astype(jnp.bfloat16)
    back = [
        (across_slots == upright(slot)).astype(jnp.float32).astype(jnp.bfloat16) for slot in slots
    ]
    first = upright(jax.nn.sigmoid(logits_ref[0, 0:1, :] - logits_ref[0, 1:2, :]))
    return pick, back, (first, 1.0 - first)


def layer_kernel(
    sizes,
    queries_ref,
    keys_ref,
    values_ref,
    out_weight_ref,
    residual_ref,
    gain_ref,
    logits_ref,
    ids_ref,
    lengths_ref,
    gate_up_hbm,
    down_hbm,
    out_ref,
    gate_up_ref,
    down_ref,
    heads_ref,
    part_ref,
    sums_ref,
    attended_ref,
    outgoing_ref,
    rows_ref,
    acts_ref,
    stage_ref,
    returned_ref,
    weight_sem,
    send_sem,
    recv_sem,
):
    n_attn, n_expert, n_hidden, n_pair, own, cap = sizes
    names = ("attn", "expert", "hidden", "pair")
    counts = (n_attn, n_expert, n_hidden, n_pair)
    me = tuple(lax.axis_index(name) for name in names)
    a, e, h, p = me
    width = rows_ref.shape[1]
    units = acts_ref.shape[2]
    columns = down_ref.shape[1]
    block = n_expert * cap
    chunk = n_hidden * block
    chunks = n_attn * n_pair
    half = chunk // 2
    pending = []

    def shifted(offset, sign=1):
        return tuple(
            lax.rem(x + (sign * d) % n, n) if d else x for x, d, n in zip(me, offset, counts)
        )

    def copy(src, dst, sem, target):
        return pltpu.make_async_remote_copy(
            src_ref=src,
            dst_ref=dst,
            send_sem=send_sem.at[sem],
            recv_sem=recv_sem.at[sem],
            device_id=dict(zip(names, target)),
            device_id_type=pl.DeviceIdType.MESH,
        )

    def send(src, dst, sem, target):
        started = copy(src, dst, sem, target)
        started.start()
        pending.append(started)

    def arrive(ref, sem):
        copy(ref, ref, sem, shifted((0, 1, 0, 0))).wait_recv()

    def at(start, size, align=16):
        return pl.ds(pl.multiple_of(start, align), size)

    weights = [
        pltpu.make_async_copy(gate_up_hbm.at[0], gate_up_ref, weight_sem.at[0]),
        pltpu.make_async_copy(down_hbm.at[0], down_ref, weight_sem.at[1]),
    ]
    for load in weights:
        load.start()

    barrier = pltpu.get_barrier_semaphore()
    others = [
        (da, de, dh, dp)
        for da in range(n_attn)
        for de in range(n_expert)
        for dh in range(n_hidden)
        for dp in range(n_pair)
        if (da, de, dh, dp) != (0, 0, 0, 0)
    ]
    for offset in others:
        pl.semaphore_signal(
            barrier,
            inc=1,
            device_id=dict(zip(names, shifted(offset))),
            device_id_type=pl.DeviceIdType.MESH,
        )
    heads_ref[...] = attend(queries_ref[0], keys_ref[0], values_ref[0], lengths_ref)
    pl.semaphore_wait(barrier, len(others))

    used = 0

    def numbers(count):
        nonlocal used
        used += count
        return used - count

    first = numbers(n_attn * n_hidden)
    mine = a * n_hidden + h
    for da in reversed(range(n_attn)):
        for dh in reversed(range(n_hidden)):
            target = shifted((da, 0, dh, 0))
            owner = target[0] * n_hidden + target[2]
            partial = jnp.dot(
                heads_ref[at(owner * own, own), :],
                out_weight_ref[...],
                preferred_element_type=jnp.float32,
            )
            if da or dh:
                slot = da * n_hidden + dh
                part_ref[slot] = partial.astype(jnp.bfloat16)
                send(part_ref.at[slot], sums_ref.at[mine], first + slot, target)
            else:
                attended_ref[...] = partial + residual_ref[0].astype(jnp.float32)
    pick, back, shares = routing(ids_ref, logits_ref, n_expert, cap)
    for da in range(n_attn):
        for dh in range(n_hidden):
            if da or dh:
                source = shifted((da, 0, dh, 0), -1)
                slot = source[0] * n_hidden + source[2]
                arrive(sums_ref.at[slot], first + da * n_hidden + dh)
                attended_ref[...] += sums_ref[slot].astype(jnp.float32)
    attended = attended_ref[...]
    scale = lax.rsqrt(jnp.mean(attended * attended, axis=1, keepdims=True) + epsilon)
    normed = (attended * scale * gain_ref[...]).astype(jnp.bfloat16)
    outgoing_ref[...] = jnp.dot(
        pick, normed, preferred_element_type=jnp.float32
    ).astype(jnp.bfloat16)

    base = ((a * n_pair + p) * n_hidden + h) * block
    first = numbers(n_expert)
    for de in reversed(range(1, n_expert)):
        target = shifted((0, de, 0, 0))
        send(
            outgoing_ref.at[at(target[1] * cap, cap)],
            rows_ref.at[at(base + e * cap, cap)],
            first + de,
            target,
        )
    rows_ref[at(base + e * cap, cap), :] = outgoing_ref[at(e * cap, cap), :]
    for de in range(1, n_expert):
        source = shifted((0, de, 0, 0), -1)
        arrive(rows_ref.at[at(base + source[1] * cap, cap)], first + de)

    steps = [(da, dp) for da in range(n_attn) for dp in range(n_pair)]
    along = numbers(chunks)
    across = numbers(chunks * n_hidden)

    def spread(step, start):
        for dh in range(1, n_hidden):
            block_ref = rows_ref.at[at(start, block)]
            send(block_ref, block_ref, across + step * n_hidden + dh, shifted((0, 0, dh, 0)))

    own_rows = rows_ref.at[at(base, block)]
    spread(0, base)
    for step, (da, dp) in enumerate(steps):
        if step:
            send(own_rows, own_rows, along + step, shifted((da, 0, 0, dp)))

    def chunk_of(step):
        da, dp = steps[step]
        source = shifted((da, 0, 0, dp), -1)
        return source[0] * n_pair + source[3]

    def forward(step):
        start = (chunk_of(step) * n_hidden + h) * block
        arrive(rows_ref.at[at(start, block)], along + step)
        spread(step, start)

    near = numbers(chunks * n_hidden * 2)
    side = numbers(chunks * n_pair * 2)
    turn_side = numbers(chunks * n_hidden * n_pair)
    turn_near = numbers(chunks * n_hidden * n_pair)
    group = h * n_pair + p

    def piece(owner, c, part):
        return acts_ref.at[owner, at(c * chunk + part * half, half)]

    def up(step):
        c = chunk_of(step)
        for dh in range(1, n_hidden):
            source = shifted((0, 0, dh, 0), -1)
            start = (c * n_hidden + source[2]) * block
            arrive(rows_ref.at[at(start, block)], across + step * n_hidden + dh)
        tile = min(256, units)

        @pl.loop(0, units // tile)
        def _(t):
            where = at(t * tile, tile, 128)
            rows = rows_ref[at(c * chunk, chunk), :]
            gate = jnp.dot(rows, gate_up_ref[0, :, where], preferred_element_type=jnp.float32)
            upward = jnp.dot(rows, gate_up_ref[1, :, where], preferred_element_type=jnp.float32)
            acts_ref[group, at(c * chunk, chunk), where] = (
                gate / (1.0 + jnp.exp(-gate)) * upward
            ).astype(jnp.bfloat16)

        for part in range(2):
            mine_ref = piece(group, c, part)
            for dh in range(1, n_hidden):
                sem = near + (c * n_hidden + dh) * 2 + part
                send(mine_ref, mine_ref, sem, shifted((0, 0, dh, 0)))
            for dp in range(1, n_pair):
                sem = side + (c * n_pair + dp) * 2 + part
                send(mine_ref, mine_ref, sem, shifted((0, 0, 0, dp)))

    def turn(step):
        c = chunk_of(step)
        for dh in range(1, n_hidden):
            owner = shifted((0, 0, dh, 0), -1)[2] * n_pair + p
            landed = piece(owner, c, 0)
            arrive(landed, near + (c * n_hidden + dh) * 2)
            for dp in range(1, n_pair):
                sem = turn_side + (c * n_hidden + dh) * n_pair + dp
                send(landed, landed, sem, shifted((0, 0, 0, dp)))
        for dp in range(1, n_pair):
            owner = h * n_pair + shifted((0, 0, 0, dp), -1)[3]
            landed = piece(owner, c, 1)
            arrive(landed, side + (c * n_pair + dp) * 2 + 1)
            for dh in range(1, n_hidden):
                sem = turn_near + (c * n_hidden + dh) * n_pair + dp
                send(landed, landed, sem, shifted((0, 0, dh, 0)))

    last = numbers(n_attn * n_expert * n_hidden * n_pair)

    def number(da, de, dh, dp):
        return last + ((da * n_expert + de) * n_hidden + dh) * n_pair + dp

    def down(step):
        c = chunk_of(step)
        for dh in range(1, n_hidden):
            owner = shifted((0, 0, dh, 0), -1)[2] * n_pair + p
            arrive(piece(owner, c, 1), near + (c * n_hidden + dh) * 2 + 1)
        for dp in range(1, n_pair):
            owner = h * n_pair + shifted((0, 0, 0, dp), -1)[3]
            arrive(piece(owner, c, 0), side + (c * n_pair + dp) * 2)
        for dh in range(1, n_hidden):
            for dp in range(1, n_pair):
                source = shifted((0, 0, dh, dp), -1)
                owner = source[2] * n_pair + source[3]
                sem = (c * n_hidden + dh) * n_pair + dp
                arrive(piece(owner, c, 0), turn_side + sem)
                arrive(piece(owner, c, 1), turn_near + sem)
        tile = min(256, columns)

        @pl.loop(0, columns // tile)
        def _(t):
            where = at(t * tile, tile, 128)
            total = jnp.zeros((chunk, tile), jnp.float32)
            for k in range(n_hidden * n_pair):
                total += jnp.dot(
                    acts_ref[k, at(c * chunk, chunk), :],
                    down_ref[k * units : (k + 1) * units, where],
                    preferred_element_type=jnp.float32,
                )
            stage_ref[at(c * chunk, chunk), where] = total.astype(jnp.bfloat16)

        da, dp = steps[step]
        for dh in range(n_hidden):
            for de in range(n_expert):
                offset = ((-da) % n_attn, de, dh, (-dp) % n_pair)
                target = shifted(offset)
                start = (c * n_hidden + target[2]) * block + target[1] * cap
                landing = (a, group, at(e * cap, cap))
                if any(offset):
                    send(
                        stage_ref.at[at(start, cap)],
                        returned_ref.at[landing],
                        number(*offset),
                        target,
                    )
                else:
                    returned_ref[landing] = stage_ref[at(start, cap), :]

    weights[0].wait()
    total_steps = len(steps)
    if total_steps > 1:
        forward(1)
    for step in range(total_steps):
        up(step)
        if step + 2 < total_steps:
            forward(step + 2)
        if step == 0:
            weights[1].wait()
        if step % n_pair == n_pair - 1 and step >= 2 * n_pair - 1:
            for earlier in range(step - 2 * n_pair + 1, step - n_pair + 1):
                turn(earlier)
    for step in range(max(0, total_steps - n_pair), total_steps):
        turn(step)
    for step in range(total_steps):
        down(step)

    for offset in others:
        source = shifted(offset, -1)
        arrive(
            returned_ref.at[
                source[0], source[2] * n_pair + source[3], at(source[1] * cap, cap)
            ],
            number(*offset),
        )
    for k in range(n_hidden * n_pair):
        where = slice(k * columns, (k + 1) * columns)
        total = returned_ref[0, k].astype(jnp.float32)
        for other in range(1, n_attn):
            total += returned_ref[other, k].astype(jnp.float32)
        rows = total.astype(jnp.bfloat16)
        sums = attended_ref[:, where]
        for choice in range(2):
            sums += shares[choice] * jnp.dot(
                back[choice], rows, preferred_element_type=jnp.float32
            )
        out_ref[0, :, where] = sums.astype(jnp.bfloat16)
    for started in pending:
        started.wait_send()


def fused_body(
    mesh,
    queries,
    keys,
    values,
    out_weight,
    residual,
    norm_gain,
    route_logits,
    expert_ids,
    doc_lengths,
    gate_up_weight,
    down_weight,
):
    n_attn, n_expert, n_hidden, n_pair = (
        mesh.shape[name] for name in ("attn", "expert", "hidden", "pair")
    )
    own, width = residual.shape[1:]
    units, columns = gate_up_weight.shape[3], down_weight.shape[2]
    cap = capacity_of(own, n_expert)
    block = n_expert * cap
    groups = n_hidden * n_pair
    slots = n_attn * groups * block
    vmem = pl.BlockSpec(memory_space=pltpu.VMEM)
    smem = pl.BlockSpec(memory_space=pltpu.SMEM)
    hbm = pl.BlockSpec(memory_space=pl.ANY)
    flops = 2 * slots * (width * 2 * units + groups * units * columns)
    return pl.pallas_call(
        functools.partial(layer_kernel, (n_attn, n_expert, n_hidden, n_pair, own, cap)),
        out_shape=jax.ShapeDtypeStruct(residual.shape, jnp.bfloat16),
        in_specs=[vmem] * 8 + [smem] + [hbm] * 2,
        out_specs=vmem,
        scratch_shapes=[
            pltpu.VMEM(gate_up_weight.shape[1:], jnp.bfloat16),
            pltpu.VMEM(down_weight.shape[1:], jnp.bfloat16),
            pltpu.VMEM(queries.shape[1:], jnp.bfloat16),
            pltpu.VMEM((n_attn * n_hidden, own, width), jnp.bfloat16),
            pltpu.VMEM((n_attn * n_hidden, own, width), jnp.bfloat16),
            pltpu.VMEM((own, width), jnp.float32),
            pltpu.VMEM((block, width), jnp.bfloat16),
            pltpu.VMEM((slots, width), jnp.bfloat16),
            pltpu.VMEM((groups, slots, units), jnp.bfloat16),
            pltpu.VMEM((slots, columns), jnp.bfloat16),
            pltpu.VMEM((n_attn, groups, block, columns), jnp.bfloat16),
            pltpu.SemaphoreType.DMA((2,)),
            pltpu.SemaphoreType.DMA((semaphores(n_attn, n_expert, n_hidden, n_pair),)),
            pltpu.SemaphoreType.DMA((semaphores(n_attn, n_expert, n_hidden, n_pair),)),
        ],
        compiler_params=pltpu.CompilerParams(
            collective_id=0, has_side_effects=True, vmem_limit_bytes=58 * 2**20
        ),
        cost_estimate=pl.CostEstimate(
            flops=flops,
            bytes_accessed=2 * (gate_up_weight.size + down_weight.size),
            transcendentals=slots * units,
        ),
    )(
        queries,
        keys,
        values,
        out_weight,
        residual,
        norm_gain[None],
        route_logits.transpose(0, 2, 1),
        expert_ids.transpose(0, 2, 1),
        doc_lengths,
        gate_up_weight,
        down_weight,
    )


def semaphores(n_attn, n_expert, n_hidden, n_pair):
    chunks = n_attn * n_pair
    return (
        n_attn * n_hidden
        + n_expert
        + chunks
        + chunks * n_hidden
        + 2 * chunks * n_hidden
        + 2 * chunks * n_pair
        + 2 * chunks * n_hidden * n_pair
        + n_attn * n_expert * n_hidden * n_pair
    )


def capacity_of(own, n_expert):
    return max(2, (2 * own + n_expert - 1) // n_expert)


def body_of(mesh, *arrays):
    own = arrays[4].shape[1]
    cap = capacity_of(own, mesh.shape["expert"])
    whole_tiles = own % 16 == 0 and cap % 16 == 0
    if whole_tiles:
        return fused_body(mesh, *arrays)
    return plain_body(*arrays)


def solution(mesh):
    in_specs = (
        P(("expert", "pair"), None, ("attn", "hidden")),
        P(("expert", "pair"), None, "attn"),
        P(("expert", "pair"), None, "attn"),
        P(("attn", "hidden"), None),
        P(("expert", "pair"), ("attn", "hidden"), None),
        P(),
        P(("expert", "pair"), ("attn", "hidden"), None),
        P(("expert", "pair"), ("attn", "hidden"), None),
        P(("expert", "pair"), None),
        P("expert", None, None, ("attn", "hidden", "pair")),
        P("expert", "attn", ("hidden", "pair")),
    )
    out_specs = P(("expert", "pair"), ("attn", "hidden"), None)
    body = functools.partial(body_of, mesh)
    return jax.shard_map(body, mesh=mesh, in_specs=in_specs, out_specs=out_specs, check_vma=False)
```

```python
import functools

import jax
import jax.numpy as jnp
from jax import lax
from jax.experimental import pallas as pl
from jax.experimental.pallas import tpu as pltpu
from jax.sharding import PartitionSpec as P

D = 4096
HD = 128


epsilon = 1e-05


def rank_rows(chosen):
    row_total = chosen.shape[-1]
    row_ids = jnp.arange(row_total, dtype=jnp.int32)
    earlier = row_ids[None, :] < row_ids[:, None]
    same_expert = chosen[..., :, None] == chosen[..., None, :]
    return jnp.sum((same_expert & earlier).astype(jnp.int32), axis=-1)


def attention(queries, keys, values, doc_lengths):
    tok_group = queries.shape[1]
    lengths = doc_lengths[0]
    order = jnp.arange(lengths.shape[0], dtype=jnp.int32)
    doc_ends = jnp.sum(jnp.where(order[None, :] <= order[:, None], lengths[None, :], 0), axis=1)
    positions = jnp.arange(tok_group, dtype=jnp.int32)
    document = jnp.sum((positions[:, None] >= doc_ends[None, :]).astype(jnp.int32), axis=1)
    allowed = (document[:, None] == document[None, :]) & (positions[None, :] <= positions[:, None])
    scores = jnp.dot(queries[0], keys[0].T, preferred_element_type=jnp.float32) * HD ** (-0.5)
    scores = jnp.where(allowed, scores, -1e30)
    row_top = jnp.max(scores, axis=1, keepdims=True)
    weights = jnp.exp(scores - row_top)
    probabilities = (weights / jnp.sum(weights, axis=1, keepdims=True)).astype(jnp.bfloat16)
    heads_out = jnp.dot(probabilities, values[0], preferred_element_type=jnp.float32).astype(
        jnp.bfloat16
    )
    return heads_out


def plain_body(
    queries,
    keys,
    values,
    out_weight,
    residual,
    norm_gain,
    route_logits,
    expert_ids,
    doc_lengths,
    gate_up_weight,
    down_weight,
):
    tok_group = queries.shape[1]
    heads_out = attention(queries, keys, values, doc_lengths)
    owned_rows = tok_group // lax.axis_size(("attn", "hidden"))
    subset = heads_out
    owned = lax.psum_scatter(
        jnp.dot(subset, out_weight, preferred_element_type=jnp.float32).astype(jnp.bfloat16),
        ("attn", "hidden"),
        scatter_dimension=0,
        tiled=True,
    ).astype(jnp.float32)
    attended = residual[0].astype(jnp.float32) + owned
    scale = lax.rsqrt(jnp.mean(attended * attended, axis=1, keepdims=True) + epsilon)
    normed = (attended * scale * norm_gain).astype(jnp.bfloat16)
    expert_count = lax.axis_size("expert")
    row_total = 2 * owned_rows
    capacity = max(2, (row_total + expert_count - 1) // expert_count)
    chosen = expert_ids[0].reshape(row_total)
    ranking = rank_rows(chosen)
    targets = jnp.arange(expert_count * capacity, dtype=jnp.int32)
    expert_of_slot = targets // capacity
    rank_of_slot = targets % capacity
    selector = (
        (chosen[None, :] == expert_of_slot[:, None]) & (ranking[None, :] == rank_of_slot[:, None])
    ).astype(jnp.bfloat16)
    repeated = jnp.repeat(normed, 2, axis=0)
    outgoing = jnp.dot(selector, repeated, preferred_element_type=jnp.float32).astype(jnp.bfloat16)
    outgoing = outgoing.reshape(expert_count, capacity, D)
    arrived = lax.all_to_all(outgoing, "expert", split_axis=0, concat_axis=0, tiled=True).reshape(
        expert_count * capacity, D
    )
    gate_up = jnp.einsum(
        "rd,gdf->rgf",
        lax.all_gather(arrived, ("attn", "hidden", "pair"), axis=0, tiled=True),
        gate_up_weight[0],
        preferred_element_type=jnp.float32,
    )
    activated = (jax.nn.silu(gate_up[:, 0]) * gate_up[:, 1]).astype(jnp.bfloat16)
    block_units = lax.all_gather(activated, ("hidden", "pair"), axis=1, tiled=True)
    down_local = down_weight[0]
    subset = block_units
    expert_out = lax.psum_scatter(
        jnp.dot(subset, down_local, preferred_element_type=jnp.float32).astype(jnp.bfloat16),
        "attn",
        scatter_dimension=0,
        tiled=True,
    )
    column_width = expert_out.shape[1]
    pair_count = lax.axis_size(("hidden", "pair"))
    tile_grid = expert_out.reshape(pair_count, expert_count, capacity, column_width)
    outgoing_wide = tile_grid.transpose(1, 0, 2, 3).reshape(
        expert_count * pair_count, 1, capacity, column_width
    )
    returned = lax.all_to_all(
        outgoing_wide, ("expert", "hidden", "pair"), split_axis=0, concat_axis=1, tiled=True
    )
    returned = returned.reshape(expert_count, pair_count, capacity, column_width).transpose(
        0, 2, 1, 3
    )
    returned = returned.reshape(expert_count * capacity, D)
    per_row = jnp.einsum(
        "sr,sd->rd", selector, returned, preferred_element_type=jnp.float32
    ).reshape(owned_rows, 2, D)
    logits = route_logits[0]
    first_share = jax.nn.sigmoid(logits[:, 0] - logits[:, 1])
    layer_out = (
        attended
        + first_share[:, None] * per_row[:, 0]
        + (1.0 - first_share)[:, None] * per_row[:, 1]
    )
    return layer_out.astype(jnp.bfloat16)[None]


def attend(queries, keys, values, lengths_ref):
    tok_group = queries.shape[0]
    places = (tok_group, tok_group)
    row, column = (lax.broadcasted_iota(jnp.int32, places, axis) for axis in range(2))
    row_document, column_document = jnp.zeros(places, jnp.int32), jnp.zeros(places, jnp.int32)
    end = 0
    for document in range(lengths_ref.shape[1]):
        end = end + lengths_ref[0, document]
        row_document += (row >= end).astype(jnp.int32)
        column_document += (column >= end).astype(jnp.int32)
    allowed = (row_document == column_document) & (column <= row)
    scores = lax.dot_general(
        queries, keys, (((1,), (1,)), ((), ())), preferred_element_type=jnp.float32
    ) * HD ** (-0.5)
    scores = jnp.where(allowed, scores, -1e30)
    weights = jnp.exp(scores - jnp.max(scores, axis=1, keepdims=True))
    probabilities = (weights / jnp.sum(weights, axis=1, keepdims=True)).astype(jnp.bfloat16)
    return jnp.dot(probabilities, values, preferred_element_type=jnp.float32).astype(
        jnp.bfloat16
    )


def routing(ids_ref, logits_ref, n_expert, cap):
    own = ids_ref.shape[2]
    block = n_expert * cap
    ids = [ids_ref[0, choice : choice + 1, :] for choice in range(2)]
    experts = lax.broadcasted_iota(jnp.int32, (max(8, n_expert), own), 0)
    named = [(experts == row).astype(jnp.float32) for row in ids]
    row, column = (lax.broadcasted_iota(jnp.int32, (own, own), axis) for axis in range(2))
    earlier = (row < column).astype(jnp.bfloat16)
    before = jnp.dot(
        (named[0] + named[1]).astype(jnp.bfloat16), earlier, preferred_element_type=jnp.float32
    )
    slots = [
        one * float(cap) + jnp.sum(before * which, axis=0, keepdims=True)
        for one, which in zip([one.astype(jnp.float32) for one in ids], named)
    ]

    def upright(values):
        return jnp.sum(jnp.where(row == column, values, 0.0), axis=1, keepdims=True)

    down_slots = lax.broadcasted_iota(jnp.int32, (block, own), 0).astype(jnp.float32)
    across_slots = lax.broadcasted_iota(jnp.int32, (own, block), 1).astype(jnp.float32)
    pick = sum((down_slots == slot).astype(jnp.float32) for slot in slots).astype(jnp.bfloat16)
    back = [
        (across_slots == upright(slot)).astype(jnp.float32).astype(jnp.bfloat16) for slot in slots
    ]
    first = upright(jax.nn.sigmoid(logits_ref[0, 0:1, :] - logits_ref[0, 1:2, :]))
    return pick, back, (first, 1.0 - first)


def layer_kernel(
    sizes,
    queries_ref,
    keys_ref,
    values_ref,
    out_weight_ref,
    residual_ref,
    gain_ref,
    logits_ref,
    ids_ref,
    lengths_ref,
    gate_up_hbm,
    down_hbm,
    out_ref,
    gate_up_ref,
    down_ref,
    heads_ref,
    part_ref,
    landed_ref,
    halfway_ref,
    sums_ref,
    attended_ref,
    outgoing_ref,
    rows_ref,
    acts_ref,
    stage_ref,
    returned_ref,
    weight_sem,
    send_sem,
    recv_sem,
):
    n_attn, n_expert, n_hidden, n_pair, own, cap = sizes
    names = ("attn", "expert", "hidden", "pair")
    counts = (n_attn, n_expert, n_hidden, n_pair)
    me = tuple(lax.axis_index(name) for name in names)
    a, e, h, p = me
    width = rows_ref.shape[1]
    units = acts_ref.shape[2]
    columns = down_ref.shape[1]
    block = n_expert * cap
    chunk = n_hidden * block
    chunks = n_attn * n_pair
    early = (chunk * 3 // 4) // 16 * 16
    pending = []

    def shifted(offset, sign=1):
        return tuple(
            lax.rem(x + (sign * d) % n, n) if d else x for x, d, n in zip(me, offset, counts)
        )

    def copy(src, dst, sem, target):
        return pltpu.make_async_remote_copy(
            src_ref=src,
            dst_ref=dst,
            send_sem=send_sem.at[sem],
            recv_sem=recv_sem.at[sem],
            device_id=dict(zip(names, target)),
            device_id_type=pl.DeviceIdType.MESH,
        )

    def send(src, dst, sem, target):
        started = copy(src, dst, sem, target)
        started.start()
        pending.append(started)

    def arrive(ref, sem):
        copy(ref, ref, sem, shifted((0, 1, 0, 0))).wait_recv()

    def at(start, size, align=16):
        return pl.ds(pl.multiple_of(start, align), size)

    weights = [
        pltpu.make_async_copy(gate_up_hbm.at[0], gate_up_ref, weight_sem.at[0]),
        pltpu.make_async_copy(down_hbm.at[0], down_ref, weight_sem.at[1]),
    ]
    for load in weights:
        load.start()

    barrier = pltpu.get_barrier_semaphore()
    others = [
        (da, de, dh, dp)
        for da in range(n_attn)
        for de in range(n_expert)
        for dh in range(n_hidden)
        for dp in range(n_pair)
        if (da, de, dh, dp) != (0, 0, 0, 0)
    ]
    for offset in others:
        pl.semaphore_signal(
            barrier,
            inc=1,
            device_id=dict(zip(names, shifted(offset))),
            device_id_type=pl.DeviceIdType.MESH,
        )
    heads_ref[...] = attend(queries_ref[0], keys_ref[0], values_ref[0], lengths_ref)
    pl.semaphore_wait(barrier, len(others))

    used = 0

    def numbers(count):
        nonlocal used
        used += count
        return used - count

    bands = 4 if width % 512 == 0 else 1
    band = width // bands
    over_hidden = numbers(bands * n_hidden)
    over_attn = numbers(bands * n_attn)

    def partial(row, column, where):
        return jnp.dot(
            heads_ref[at((row * n_hidden + column) * own, own), :],
            out_weight_ref[:, where],
            preferred_element_type=jnp.float32,
        )

    places = [slice(j * band, (j + 1) * band) for j in range(bands)]
    for j, where in enumerate(places):
        for dh in range(1, n_hidden):
            target = shifted((0, 0, dh, 0))
            for row in range(n_attn):
                part_ref[dh, row * own : (row + 1) * own, where] = partial(
                    row, target[2], where
                ).astype(jnp.bfloat16)
            send(
                part_ref.at[dh, :, where],
                landed_ref.at[h, :, where],
                over_hidden + j * n_hidden + dh,
                target,
            )
    pick, back, shares = routing(ids_ref, logits_ref, n_expert, cap)
    for j, where in enumerate(places):
        for dh in range(1, n_hidden):
            source = shifted((0, 0, dh, 0), -1)
            arrive(landed_ref.at[source[2], :, where], over_hidden + j * n_hidden + dh)
        for da in reversed(range(n_attn)):
            target = shifted((da, 0, 0, 0))
            total = partial(target[0], h, where)
            for dh in range(1, n_hidden):
                source = shifted((0, 0, dh, 0), -1)
                total += landed_ref[source[2], at(target[0] * own, own), where].astype(
                    jnp.float32
                )
            if da:
                halfway_ref[da, :, where] = total.astype(jnp.bfloat16)
                send(
                    halfway_ref.at[da, :, where],
                    sums_ref.at[a, :, where],
                    over_attn + j * n_attn + da,
                    target,
                )
            else:
                attended_ref[:, where] = total + residual_ref[0, :, where].astype(jnp.float32)
    for j, where in enumerate(places):
        for da in range(1, n_attn):
            source = shifted((da, 0, 0, 0), -1)
            arrive(sums_ref.at[source[0], :, where], over_attn + j * n_attn + da)
            attended_ref[:, where] += sums_ref[source[0], :, where].astype(jnp.float32)
    attended = attended_ref[...]
    scale = lax.rsqrt(jnp.mean(attended * attended, axis=1, keepdims=True) + epsilon)
    normed = (attended * scale * gain_ref[...]).astype(jnp.bfloat16)
    outgoing_ref[...] = jnp.dot(
        pick, normed, preferred_element_type=jnp.float32
    ).astype(jnp.bfloat16)

    base = ((a * n_pair + p) * n_hidden + h) * block
    first = numbers(n_expert)
    for de in reversed(range(1, n_expert)):
        target = shifted((0, de, 0, 0))
        send(
            outgoing_ref.at[at(target[1] * cap, cap)],
            rows_ref.at[at(base + e * cap, cap)],
            first + de,
            target,
        )
    rows_ref[at(base + e * cap, cap), :] = outgoing_ref[at(e * cap, cap), :]
    for de in range(1, n_expert):
        source = shifted((0, de, 0, 0), -1)
        arrive(rows_ref.at[at(base + source[1] * cap, cap)], first + de)

    steps = [(da, dp) for da in reversed(range(n_attn)) for dp in reversed(range(n_pair))]
    along = numbers(chunks)
    across = numbers(chunks * n_hidden)

    def spread(step, start):
        for dh in range(1, n_hidden):
            block_ref = rows_ref.at[at(start, block)]
            send(block_ref, block_ref, across + step * n_hidden + dh, shifted((0, 0, dh, 0)))

    own_rows = rows_ref.at[at(base, block)]
    spread(chunks - 1, base)
    for step, (da, dp) in enumerate(steps):
        if da or dp:
            send(own_rows, own_rows, along + step, shifted((da, 0, 0, dp)))

    def chunk_of(step):
        da, dp = steps[step]
        source = shifted((da, 0, 0, dp), -1)
        return source[0] * n_pair + source[3]

    def forward(step):
        start = (chunk_of(step) * n_hidden + h) * block
        arrive(rows_ref.at[at(start, block)], along + step)
        spread(step, start)

    near = numbers(chunks * n_hidden * 2)
    side = numbers(chunks * n_pair * 2)
    turn_side = numbers(chunks * n_hidden * n_pair)
    turn_near = numbers(chunks * n_hidden * n_pair)
    group = h * n_pair + p

    def piece(owner, c, part):
        return acts_ref.at[owner, at(c * chunk + part * early, chunk - early if part else early)]

    def up(step):
        c = chunk_of(step)
        for dh in range(1, n_hidden):
            source = shifted((0, 0, dh, 0), -1)
            start = (c * n_hidden + source[2]) * block
            arrive(rows_ref.at[at(start, block)], across + step * n_hidden + dh)
        tile = min(256, units)

        @pl.loop(0, units // tile)
        def _(t):
            where = at(t * tile, tile, 128)
            rows = rows_ref[at(c * chunk, chunk), :]
            gate = jnp.dot(rows, gate_up_ref[0, :, where], preferred_element_type=jnp.float32)
            upward = jnp.dot(rows, gate_up_ref[1, :, where], preferred_element_type=jnp.float32)
            acts_ref[group, at(c * chunk, chunk), where] = (
                gate / (1.0 + jnp.exp(-gate)) * upward
            ).astype(jnp.bfloat16)

        for part in range(2):
            mine_ref = piece(group, c, part)
            for dh in range(1, n_hidden):
                sem = near + (c * n_hidden + dh) * 2 + part
                send(mine_ref, mine_ref, sem, shifted((0, 0, dh, 0)))
            for dp in range(1, n_pair):
                sem = side + (c * n_pair + dp) * 2 + part
                send(mine_ref, mine_ref, sem, shifted((0, 0, 0, dp)))

    def turn(step):
        c = chunk_of(step)
        for dh in range(1, n_hidden):
            owner = shifted((0, 0, dh, 0), -1)[2] * n_pair + p
            landed = piece(owner, c, 0)
            arrive(landed, near + (c * n_hidden + dh) * 2)
            for dp in range(1, n_pair):
                sem = turn_side + (c * n_hidden + dh) * n_pair + dp
                send(landed, landed, sem, shifted((0, 0, 0, dp)))
        for dp in range(1, n_pair):
            owner = h * n_pair + shifted((0, 0, 0, dp), -1)[3]
            landed = piece(owner, c, 1)
            arrive(landed, side + (c * n_pair + dp) * 2 + 1)
            for dh in range(1, n_hidden):
                sem = turn_near + (c * n_hidden + dh) * n_pair + dp
                send(landed, landed, sem, shifted((0, 0, dh, 0)))

    last = numbers(n_attn * n_expert * n_hidden * n_pair)

    def number(da, de, dh, dp):
        return last + ((da * n_expert + de) * n_hidden + dh) * n_pair + dp

    def down(step):
        c = chunk_of(step)
        for dh in range(1, n_hidden):
            owner = shifted((0, 0, dh, 0), -1)[2] * n_pair + p
            arrive(piece(owner, c, 1), near + (c * n_hidden + dh) * 2 + 1)
        for dp in range(1, n_pair):
            owner = h * n_pair + shifted((0, 0, 0, dp), -1)[3]
            arrive(piece(owner, c, 0), side + (c * n_pair + dp) * 2)
        for dh in range(1, n_hidden):
            for dp in range(1, n_pair):
                source = shifted((0, 0, dh, dp), -1)
                owner = source[2] * n_pair + source[3]
                sem = (c * n_hidden + dh) * n_pair + dp
                arrive(piece(owner, c, 0), turn_side + sem)
                arrive(piece(owner, c, 1), turn_near + sem)
        tile = min(256, columns)

        @pl.loop(0, columns // tile)
        def _(t):
            where = at(t * tile, tile, 128)
            total = jnp.zeros((chunk, tile), jnp.float32)
            for k in range(n_hidden * n_pair):
                total += jnp.dot(
                    acts_ref[k, at(c * chunk, chunk), :],
                    down_ref[k * units : (k + 1) * units, where],
                    preferred_element_type=jnp.float32,
                )
            stage_ref[at(c * chunk, chunk), where] = total.astype(jnp.bfloat16)

        da, dp = steps[step]
        for dh in range(n_hidden):
            for de in range(n_expert):
                offset = ((-da) % n_attn, de, dh, (-dp) % n_pair)
                target = shifted(offset)
                start = (c * n_hidden + target[2]) * block + target[1] * cap
                landing = (a, group, at(e * cap, cap))
                if any(offset):
                    send(
                        stage_ref.at[at(start, cap)],
                        returned_ref.at[landing],
                        number(*offset),
                        target,
                    )
                else:
                    returned_ref[landing] = stage_ref[at(start, cap), :]

    weights[0].wait()
    for step in range(chunks - 1):
        if step < 2:
            forward(step)
    for step in range(chunks):
        up(step)
        if step + 2 < chunks - 1:
            forward(step + 2)
    weights[1].wait()
    for step in range(chunks):
        turn(step)
        if step >= n_pair:
            down(step - n_pair)
    for step in range(max(0, chunks - n_pair), chunks):
        down(step)

    for offset in others:
        source = shifted(offset, -1)
        arrive(
            returned_ref.at[
                source[0], source[2] * n_pair + source[3], at(source[1] * cap, cap)
            ],
            number(*offset),
        )
    for k in range(n_hidden * n_pair):
        where = slice(k * columns, (k + 1) * columns)
        total = returned_ref[0, k].astype(jnp.float32)
        for other in range(1, n_attn):
            total += returned_ref[other, k].astype(jnp.float32)
        rows = total.astype(jnp.bfloat16)
        sums = attended_ref[:, where]
        for choice in range(2):
            sums += shares[choice] * jnp.dot(
                back[choice], rows, preferred_element_type=jnp.float32
            )
        out_ref[0, :, where] = sums.astype(jnp.bfloat16)
    for started in pending:
        started.wait_send()


def fused_body(
    mesh,
    queries,
    keys,
    values,
    out_weight,
    residual,
    norm_gain,
    route_logits,
    expert_ids,
    doc_lengths,
    gate_up_weight,
    down_weight,
):
    n_attn, n_expert, n_hidden, n_pair = (
        mesh.shape[name] for name in ("attn", "expert", "hidden", "pair")
    )
    own, width = residual.shape[1:]
    units, columns = gate_up_weight.shape[3], down_weight.shape[2]
    cap = capacity_of(own, n_expert)
    block = n_expert * cap
    groups = n_hidden * n_pair
    slots = n_attn * groups * block
    vmem = pl.BlockSpec(memory_space=pltpu.VMEM)
    smem = pl.BlockSpec(memory_space=pltpu.SMEM)
    hbm = pl.BlockSpec(memory_space=pl.ANY)
    flops = 2 * slots * (width * 2 * units + groups * units * columns)
    return pl.pallas_call(
        functools.partial(layer_kernel, (n_attn, n_expert, n_hidden, n_pair, own, cap)),
        out_shape=jax.ShapeDtypeStruct(residual.shape, jnp.bfloat16),
        in_specs=[vmem] * 8 + [smem] + [hbm] * 2,
        out_specs=vmem,
        scratch_shapes=[
            pltpu.VMEM(gate_up_weight.shape[1:], jnp.bfloat16),
            pltpu.VMEM(down_weight.shape[1:], jnp.bfloat16),
            pltpu.VMEM(queries.shape[1:], jnp.bfloat16),
            pltpu.VMEM((n_hidden, n_attn * own, width), jnp.bfloat16),
            pltpu.VMEM((n_hidden, n_attn * own, width), jnp.bfloat16),
            pltpu.VMEM((n_attn, own, width), jnp.bfloat16),
            pltpu.VMEM((n_attn, own, width), jnp.bfloat16),
            pltpu.VMEM((own, width), jnp.float32),
            pltpu.VMEM((block, width), jnp.bfloat16),
            pltpu.VMEM((slots, width), jnp.bfloat16),
            pltpu.VMEM((groups, slots, units), jnp.bfloat16),
            pltpu.VMEM((slots, columns), jnp.bfloat16),
            pltpu.VMEM((n_attn, groups, block, columns), jnp.bfloat16),
            pltpu.SemaphoreType.DMA((2,)),
            pltpu.SemaphoreType.DMA((semaphores(n_attn, n_expert, n_hidden, n_pair),)),
            pltpu.SemaphoreType.DMA((semaphores(n_attn, n_expert, n_hidden, n_pair),)),
        ],
        compiler_params=pltpu.CompilerParams(
            collective_id=0, has_side_effects=True, vmem_limit_bytes=58 * 2**20
        ),
        cost_estimate=pl.CostEstimate(
            flops=flops,
            bytes_accessed=2 * (gate_up_weight.size + down_weight.size),
            transcendentals=slots * units,
        ),
    )(
        queries,
        keys,
        values,
        out_weight,
        residual,
        norm_gain[None],
        route_logits.transpose(0, 2, 1),
        expert_ids.transpose(0, 2, 1),
        doc_lengths,
        gate_up_weight,
        down_weight,
    )


def semaphores(n_attn, n_expert, n_hidden, n_pair):
    chunks = n_attn * n_pair
    return (
        4 * n_hidden
        + 4 * n_attn
        + n_expert
        + chunks
        + chunks * n_hidden
        + 2 * chunks * n_hidden
        + 2 * chunks * n_pair
        + 2 * chunks * n_hidden * n_pair
        + n_attn * n_expert * n_hidden * n_pair
    )


def capacity_of(own, n_expert):
    return max(2, (2 * own + n_expert - 1) // n_expert)


def body_of(mesh, *arrays):
    own = arrays[4].shape[1]
    cap = capacity_of(own, mesh.shape["expert"])
    whole_tiles = own % 16 == 0 and cap % 16 == 0
    if whole_tiles:
        return fused_body(mesh, *arrays)
    return plain_body(*arrays)


def solution(mesh):
    in_specs = (
        P(("expert", "pair"), None, ("attn", "hidden")),
        P(("expert", "pair"), None, "attn"),
        P(("expert", "pair"), None, "attn"),
        P(("attn", "hidden"), None),
        P(("expert", "pair"), ("attn", "hidden"), None),
        P(),
        P(("expert", "pair"), ("attn", "hidden"), None),
        P(("expert", "pair"), ("attn", "hidden"), None),
        P(("expert", "pair"), None),
        P("expert", None, None, ("attn", "hidden", "pair")),
        P("expert", "attn", ("hidden", "pair")),
    )
    out_specs = P(("expert", "pair"), ("attn", "hidden"), None)
    body = functools.partial(body_of, mesh)
    return jax.shard_map(body, mesh=mesh, in_specs=in_specs, out_specs=out_specs, check_vma=False)
```

```python
import functools

import jax
import jax.numpy as jnp
from jax import lax
from jax.experimental import pallas as pl
from jax.experimental.pallas import tpu as pltpu
from jax.sharding import PartitionSpec as P

D = 4096
HD = 128


epsilon = 1e-05


def rank_rows(chosen):
    row_total = chosen.shape[-1]
    row_ids = jnp.arange(row_total, dtype=jnp.int32)
    earlier = row_ids[None, :] < row_ids[:, None]
    same_expert = chosen[..., :, None] == chosen[..., None, :]
    return jnp.sum((same_expert & earlier).astype(jnp.int32), axis=-1)


def attention(queries, keys, values, doc_lengths):
    tok_group = queries.shape[1]
    lengths = doc_lengths[0]
    order = jnp.arange(lengths.shape[0], dtype=jnp.int32)
    doc_ends = jnp.sum(jnp.where(order[None, :] <= order[:, None], lengths[None, :], 0), axis=1)
    positions = jnp.arange(tok_group, dtype=jnp.int32)
    document = jnp.sum((positions[:, None] >= doc_ends[None, :]).astype(jnp.int32), axis=1)
    allowed = (document[:, None] == document[None, :]) & (positions[None, :] <= positions[:, None])
    scores = jnp.dot(queries[0], keys[0].T, preferred_element_type=jnp.float32) * HD ** (-0.5)
    scores = jnp.where(allowed, scores, -1e30)
    row_top = jnp.max(scores, axis=1, keepdims=True)
    weights = jnp.exp(scores - row_top)
    probabilities = (weights / jnp.sum(weights, axis=1, keepdims=True)).astype(jnp.bfloat16)
    heads_out = jnp.dot(probabilities, values[0], preferred_element_type=jnp.float32).astype(
        jnp.bfloat16
    )
    return heads_out


def plain_body(
    queries,
    keys,
    values,
    out_weight,
    residual,
    norm_gain,
    route_logits,
    expert_ids,
    doc_lengths,
    gate_up_weight,
    down_weight,
):
    tok_group = queries.shape[1]
    heads_out = attention(queries, keys, values, doc_lengths)
    owned_rows = tok_group // lax.axis_size(("attn", "hidden"))
    subset = heads_out
    owned = lax.psum_scatter(
        jnp.dot(subset, out_weight, preferred_element_type=jnp.float32).astype(jnp.bfloat16),
        ("attn", "hidden"),
        scatter_dimension=0,
        tiled=True,
    ).astype(jnp.float32)
    attended = residual[0].astype(jnp.float32) + owned
    scale = lax.rsqrt(jnp.mean(attended * attended, axis=1, keepdims=True) + epsilon)
    normed = (attended * scale * norm_gain).astype(jnp.bfloat16)
    expert_count = lax.axis_size("expert")
    row_total = 2 * owned_rows
    capacity = max(2, (row_total + expert_count - 1) // expert_count)
    chosen = expert_ids[0].reshape(row_total)
    ranking = rank_rows(chosen)
    targets = jnp.arange(expert_count * capacity, dtype=jnp.int32)
    expert_of_slot = targets // capacity
    rank_of_slot = targets % capacity
    selector = (
        (chosen[None, :] == expert_of_slot[:, None]) & (ranking[None, :] == rank_of_slot[:, None])
    ).astype(jnp.bfloat16)
    repeated = jnp.repeat(normed, 2, axis=0)
    outgoing = jnp.dot(selector, repeated, preferred_element_type=jnp.float32).astype(jnp.bfloat16)
    outgoing = outgoing.reshape(expert_count, capacity, D)
    arrived = lax.all_to_all(outgoing, "expert", split_axis=0, concat_axis=0, tiled=True).reshape(
        expert_count * capacity, D
    )
    gate_up = jnp.einsum(
        "rd,gdf->rgf",
        lax.all_gather(arrived, ("attn", "hidden", "pair"), axis=0, tiled=True),
        gate_up_weight[0],
        preferred_element_type=jnp.float32,
    )
    activated = (jax.nn.silu(gate_up[:, 0]) * gate_up[:, 1]).astype(jnp.bfloat16)
    block_units = lax.all_gather(activated, ("hidden", "pair"), axis=1, tiled=True)
    down_local = down_weight[0]
    subset = block_units
    expert_out = lax.psum_scatter(
        jnp.dot(subset, down_local, preferred_element_type=jnp.float32).astype(jnp.bfloat16),
        "attn",
        scatter_dimension=0,
        tiled=True,
    )
    column_width = expert_out.shape[1]
    pair_count = lax.axis_size(("hidden", "pair"))
    tile_grid = expert_out.reshape(pair_count, expert_count, capacity, column_width)
    outgoing_wide = tile_grid.transpose(1, 0, 2, 3).reshape(
        expert_count * pair_count, 1, capacity, column_width
    )
    returned = lax.all_to_all(
        outgoing_wide, ("expert", "hidden", "pair"), split_axis=0, concat_axis=1, tiled=True
    )
    returned = returned.reshape(expert_count, pair_count, capacity, column_width).transpose(
        0, 2, 1, 3
    )
    returned = returned.reshape(expert_count * capacity, D)
    per_row = jnp.einsum(
        "sr,sd->rd", selector, returned, preferred_element_type=jnp.float32
    ).reshape(owned_rows, 2, D)
    logits = route_logits[0]
    first_share = jax.nn.sigmoid(logits[:, 0] - logits[:, 1])
    layer_out = (
        attended
        + first_share[:, None] * per_row[:, 0]
        + (1.0 - first_share)[:, None] * per_row[:, 1]
    )
    return layer_out.astype(jnp.bfloat16)[None]


def attend(queries, keys, values, lengths_ref):
    tok_group = queries.shape[0]
    places = (tok_group, tok_group)
    row, column = (lax.broadcasted_iota(jnp.int32, places, axis) for axis in range(2))
    row_document, column_document = jnp.zeros(places, jnp.int32), jnp.zeros(places, jnp.int32)
    end = 0
    for document in range(lengths_ref.shape[1]):
        end = end + lengths_ref[0, document]
        row_document += (row >= end).astype(jnp.int32)
        column_document += (column >= end).astype(jnp.int32)
    allowed = (row_document == column_document) & (column <= row)
    scores = lax.dot_general(
        queries, keys, (((1,), (1,)), ((), ())), preferred_element_type=jnp.float32
    ) * HD ** (-0.5)
    scores = jnp.where(allowed, scores, -1e30)
    weights = jnp.exp(scores - jnp.max(scores, axis=1, keepdims=True))
    probabilities = (weights / jnp.sum(weights, axis=1, keepdims=True)).astype(jnp.bfloat16)
    return jnp.dot(probabilities, values, preferred_element_type=jnp.float32).astype(
        jnp.bfloat16
    )


def routing(ids_ref, logits_ref, n_expert, cap):
    own = ids_ref.shape[2]
    block = n_expert * cap
    ids = [ids_ref[0, choice : choice + 1, :] for choice in range(2)]
    experts = lax.broadcasted_iota(jnp.int32, (max(8, n_expert), own), 0)
    named = [(experts == row).astype(jnp.float32) for row in ids]
    row, column = (lax.broadcasted_iota(jnp.int32, (own, own), axis) for axis in range(2))
    earlier = (row < column).astype(jnp.bfloat16)
    before = jnp.dot(
        (named[0] + named[1]).astype(jnp.bfloat16), earlier, preferred_element_type=jnp.float32
    )
    slots = [
        one * float(cap) + jnp.sum(before * which, axis=0, keepdims=True)
        for one, which in zip([one.astype(jnp.float32) for one in ids], named)
    ]

    def upright(values):
        return jnp.sum(jnp.where(row == column, values, 0.0), axis=1, keepdims=True)

    down_slots = lax.broadcasted_iota(jnp.int32, (block, own), 0).astype(jnp.float32)
    across_slots = lax.broadcasted_iota(jnp.int32, (own, block), 1).astype(jnp.float32)
    pick = sum((down_slots == slot).astype(jnp.float32) for slot in slots).astype(jnp.bfloat16)
    back = [
        (across_slots == upright(slot)).astype(jnp.float32).astype(jnp.bfloat16) for slot in slots
    ]
    first = upright(jax.nn.sigmoid(logits_ref[0, 0:1, :] - logits_ref[0, 1:2, :]))
    return pick, back, (first, 1.0 - first)


def layer_kernel(
    sizes,
    queries_ref,
    keys_ref,
    values_ref,
    out_weight_ref,
    residual_ref,
    gain_ref,
    logits_ref,
    ids_ref,
    lengths_ref,
    gate_up_hbm,
    down_hbm,
    out_ref,
    gate_up_ref,
    down_ref,
    heads_ref,
    part_ref,
    landed_ref,
    halfway_ref,
    sums_ref,
    attended_ref,
    outgoing_ref,
    rows_ref,
    acts_ref,
    stage_ref,
    returned_ref,
    weight_sem,
    send_sem,
    recv_sem,
):
    n_attn, n_expert, n_hidden, n_pair, own, cap = sizes
    names = ("attn", "expert", "hidden", "pair")
    counts = (n_attn, n_expert, n_hidden, n_pair)
    me = tuple(lax.axis_index(name) for name in names)
    a, e, h, p = me
    width = rows_ref.shape[1]
    units = acts_ref.shape[2]
    columns = down_ref.shape[1]
    block = n_expert * cap
    chunk = n_hidden * block
    chunks = n_attn * n_pair
    half = chunk // 2
    pending = []

    def shifted(offset, sign=1):
        return tuple(
            lax.rem(x + (sign * d) % n, n) if d else x for x, d, n in zip(me, offset, counts)
        )

    def copy(src, dst, sem, target):
        return pltpu.make_async_remote_copy(
            src_ref=src,
            dst_ref=dst,
            send_sem=send_sem.at[sem],
            recv_sem=recv_sem.at[sem],
            device_id=dict(zip(names, target)),
            device_id_type=pl.DeviceIdType.MESH,
        )

    def send(src, dst, sem, target):
        started = copy(src, dst, sem, target)
        started.start()
        pending.append(started)

    def arrive(ref, sem):
        copy(ref, ref, sem, shifted((0, 1, 0, 0))).wait_recv()

    def at(start, size, align=16):
        return pl.ds(pl.multiple_of(start, align), size)

    weights = [
        pltpu.make_async_copy(gate_up_hbm.at[0], gate_up_ref, weight_sem.at[0]),
        pltpu.make_async_copy(down_hbm.at[0], down_ref, weight_sem.at[1]),
    ]
    for load in weights:
        load.start()

    barrier = pltpu.get_barrier_semaphore()
    others = [
        (da, de, dh, dp)
        for da in range(n_attn)
        for de in range(n_expert)
        for dh in range(n_hidden)
        for dp in range(n_pair)
        if (da, de, dh, dp) != (0, 0, 0, 0)
    ]
    for offset in others:
        pl.semaphore_signal(
            barrier,
            inc=1,
            device_id=dict(zip(names, shifted(offset))),
            device_id_type=pl.DeviceIdType.MESH,
        )
    heads_ref[...] = attend(queries_ref[0], keys_ref[0], values_ref[0], lengths_ref)
    pl.semaphore_wait(barrier, len(others))

    used = 0

    def numbers(count):
        nonlocal used
        used += count
        return used - count

    bands = 4 if width % 512 == 0 else 1
    band = width // bands
    over_hidden = numbers(bands * n_hidden)
    over_attn = numbers(bands * n_attn)

    def partial(row, column, where):
        return jnp.dot(
            heads_ref[at((row * n_hidden + column) * own, own), :],
            out_weight_ref[:, where],
            preferred_element_type=jnp.float32,
        )

    places = [slice(j * band, (j + 1) * band) for j in range(bands)]
    for j, where in enumerate(places):
        for dh in range(1, n_hidden):
            target = shifted((0, 0, dh, 0))
            for row in range(n_attn):
                part_ref[dh, row * own : (row + 1) * own, where] = partial(
                    row, target[2], where
                ).astype(jnp.bfloat16)
            send(
                part_ref.at[dh, :, where],
                landed_ref.at[h, :, where],
                over_hidden + j * n_hidden + dh,
                target,
            )
    pick, back, shares = routing(ids_ref, logits_ref, n_expert, cap)
    for j, where in enumerate(places):
        for dh in range(1, n_hidden):
            source = shifted((0, 0, dh, 0), -1)
            arrive(landed_ref.at[source[2], :, where], over_hidden + j * n_hidden + dh)
        for da in reversed(range(n_attn)):
            target = shifted((da, 0, 0, 0))
            total = partial(target[0], h, where)
            for dh in range(1, n_hidden):
                source = shifted((0, 0, dh, 0), -1)
                total += landed_ref[source[2], at(target[0] * own, own), where].astype(
                    jnp.float32
                )
            if da:
                halfway_ref[da, :, where] = total.astype(jnp.bfloat16)
                send(
                    halfway_ref.at[da, :, where],
                    sums_ref.at[a, :, where],
                    over_attn + j * n_attn + da,
                    target,
                )
            else:
                attended_ref[:, where] = total + residual_ref[0, :, where].astype(jnp.float32)
    for j, where in enumerate(places):
        for da in range(1, n_attn):
            source = shifted((da, 0, 0, 0), -1)
            arrive(sums_ref.at[source[0], :, where], over_attn + j * n_attn + da)
            attended_ref[:, where] += sums_ref[source[0], :, where].astype(jnp.float32)
    attended = attended_ref[...]
    scale = lax.rsqrt(jnp.mean(attended * attended, axis=1, keepdims=True) + epsilon)
    normed = (attended * scale * gain_ref[...]).astype(jnp.bfloat16)
    outgoing_ref[...] = jnp.dot(
        pick, normed, preferred_element_type=jnp.float32
    ).astype(jnp.bfloat16)

    base = ((a * n_pair + p) * n_hidden + h) * block
    first = numbers(n_expert)
    for de in reversed(range(1, n_expert)):
        target = shifted((0, de, 0, 0))
        send(
            outgoing_ref.at[at(target[1] * cap, cap)],
            rows_ref.at[at(base + e * cap, cap)],
            first + de,
            target,
        )
    rows_ref[at(base + e * cap, cap), :] = outgoing_ref[at(e * cap, cap), :]
    for de in range(1, n_expert):
        source = shifted((0, de, 0, 0), -1)
        arrive(rows_ref.at[at(base + source[1] * cap, cap)], first + de)

    steps = [(da, dp) for da in range(n_attn) for dp in range(n_pair)]
    along = numbers(chunks)
    across = numbers(chunks * n_hidden)

    def spread(step, start):
        for dh in range(1, n_hidden):
            block_ref = rows_ref.at[at(start, block)]
            send(block_ref, block_ref, across + step * n_hidden + dh, shifted((0, 0, dh, 0)))

    own_rows = rows_ref.at[at(base, block)]
    spread(0, base)
    for step, (da, dp) in enumerate(steps):
        if step:
            send(own_rows, own_rows, along + step, shifted((da, 0, 0, dp)))

    def chunk_of(step):
        da, dp = steps[step]
        source = shifted((da, 0, 0, dp), -1)
        return source[0] * n_pair + source[3]

    def forward(step):
        start = (chunk_of(step) * n_hidden + h) * block
        arrive(rows_ref.at[at(start, block)], along + step)
        spread(step, start)

    near = numbers(chunks * n_hidden * 2)
    side = numbers(chunks * n_pair * 2)
    turn_side = numbers(chunks * n_hidden * n_pair)
    turn_near = numbers(chunks * n_hidden * n_pair)
    group = h * n_pair + p

    def piece(owner, c, part):
        return acts_ref.at[owner, at(c * chunk + part * half, half)]

    def up(step):
        c = chunk_of(step)
        for dh in range(1, n_hidden):
            source = shifted((0, 0, dh, 0), -1)
            start = (c * n_hidden + source[2]) * block
            arrive(rows_ref.at[at(start, block)], across + step * n_hidden + dh)
        tile = min(256, units)

        @pl.loop(0, units // tile)
        def _(t):
            where = at(t * tile, tile, 128)
            rows = rows_ref[at(c * chunk, chunk), :]
            gate = jnp.dot(rows, gate_up_ref[0, :, where], preferred_element_type=jnp.float32)
            upward = jnp.dot(rows, gate_up_ref[1, :, where], preferred_element_type=jnp.float32)
            acts_ref[group, at(c * chunk, chunk), where] = (
                gate / (1.0 + jnp.exp(-gate)) * upward
            ).astype(jnp.bfloat16)

        for part in range(2):
            mine_ref = piece(group, c, part)
            for dh in range(1, n_hidden):
                sem = near + (c * n_hidden + dh) * 2 + part
                send(mine_ref, mine_ref, sem, shifted((0, 0, dh, 0)))
            for dp in range(1, n_pair):
                sem = side + (c * n_pair + dp) * 2 + part
                send(mine_ref, mine_ref, sem, shifted((0, 0, 0, dp)))

    def turn(step):
        c = chunk_of(step)
        for dh in range(1, n_hidden):
            owner = shifted((0, 0, dh, 0), -1)[2] * n_pair + p
            landed = piece(owner, c, 0)
            arrive(landed, near + (c * n_hidden + dh) * 2)
            for dp in range(1, n_pair):
                sem = turn_side + (c * n_hidden + dh) * n_pair + dp
                send(landed, landed, sem, shifted((0, 0, 0, dp)))
        for dp in range(1, n_pair):
            owner = h * n_pair + shifted((0, 0, 0, dp), -1)[3]
            landed = piece(owner, c, 1)
            arrive(landed, side + (c * n_pair + dp) * 2 + 1)
            for dh in range(1, n_hidden):
                sem = turn_near + (c * n_hidden + dh) * n_pair + dp
                send(landed, landed, sem, shifted((0, 0, dh, 0)))

    last = numbers(n_attn * n_expert * n_hidden * n_pair)

    def number(da, de, dh, dp):
        return last + ((da * n_expert + de) * n_hidden + dh) * n_pair + dp

    def down(step):
        c = chunk_of(step)
        for dh in range(1, n_hidden):
            owner = shifted((0, 0, dh, 0), -1)[2] * n_pair + p
            arrive(piece(owner, c, 1), near + (c * n_hidden + dh) * 2 + 1)
        for dp in range(1, n_pair):
            owner = h * n_pair + shifted((0, 0, 0, dp), -1)[3]
            arrive(piece(owner, c, 0), side + (c * n_pair + dp) * 2)
        for dh in range(1, n_hidden):
            for dp in range(1, n_pair):
                source = shifted((0, 0, dh, dp), -1)
                owner = source[2] * n_pair + source[3]
                sem = (c * n_hidden + dh) * n_pair + dp
                arrive(piece(owner, c, 0), turn_side + sem)
                arrive(piece(owner, c, 1), turn_near + sem)
        tile = min(256, columns)

        @pl.loop(0, columns // tile)
        def _(t):
            where = at(t * tile, tile, 128)
            total = jnp.zeros((chunk, tile), jnp.float32)
            for k in range(n_hidden * n_pair):
                total += jnp.dot(
                    acts_ref[k, at(c * chunk, chunk), :],
                    down_ref[k * units : (k + 1) * units, where],
                    preferred_element_type=jnp.float32,
                )
            stage_ref[at(c * chunk, chunk), where] = total.astype(jnp.bfloat16)

        da, dp = steps[step]
        for dh in range(n_hidden):
            for de in range(n_expert):
                offset = ((-da) % n_attn, de, dh, (-dp) % n_pair)
                target = shifted(offset)
                start = (c * n_hidden + target[2]) * block + target[1] * cap
                landing = (a, group, at(e * cap, cap))
                if any(offset):
                    send(
                        stage_ref.at[at(start, cap)],
                        returned_ref.at[landing],
                        number(*offset),
                        target,
                    )
                else:
                    returned_ref[landing] = stage_ref[at(start, cap), :]

    weights[0].wait()
    total_steps = len(steps)
    if total_steps > 1:
        forward(1)
    for step in range(total_steps):
        up(step)
        if step + 2 < total_steps:
            forward(step + 2)
        if step == 0:
            weights[1].wait()
        if step % n_pair == n_pair - 1 and step >= 2 * n_pair - 1:
            for earlier in range(step - 2 * n_pair + 1, step - n_pair + 1):
                turn(earlier)
    for step in range(max(0, total_steps - n_pair), total_steps):
        turn(step)
    for step in range(total_steps):
        down(step)

    for offset in others:
        source = shifted(offset, -1)
        arrive(
            returned_ref.at[
                source[0], source[2] * n_pair + source[3], at(source[1] * cap, cap)
            ],
            number(*offset),
        )
    for k in range(n_hidden * n_pair):
        where = slice(k * columns, (k + 1) * columns)
        total = returned_ref[0, k].astype(jnp.float32)
        for other in range(1, n_attn):
            total += returned_ref[other, k].astype(jnp.float32)
        rows = total.astype(jnp.bfloat16)
        sums = attended_ref[:, where]
        for choice in range(2):
            sums += shares[choice] * jnp.dot(
                back[choice], rows, preferred_element_type=jnp.float32
            )
        out_ref[0, :, where] = sums.astype(jnp.bfloat16)
    for started in pending:
        started.wait_send()


def fused_body(
    mesh,
    queries,
    keys,
    values,
    out_weight,
    residual,
    norm_gain,
    route_logits,
    expert_ids,
    doc_lengths,
    gate_up_weight,
    down_weight,
):
    n_attn, n_expert, n_hidden, n_pair = (
        mesh.shape[name] for name in ("attn", "expert", "hidden", "pair")
    )
    own, width = residual.shape[1:]
    units, columns = gate_up_weight.shape[3], down_weight.shape[2]
    cap = capacity_of(own, n_expert)
    block = n_expert * cap
    groups = n_hidden * n_pair
    slots = n_attn * groups * block
    vmem = pl.BlockSpec(memory_space=pltpu.VMEM)
    smem = pl.BlockSpec(memory_space=pltpu.SMEM)
    hbm = pl.BlockSpec(memory_space=pl.ANY)
    flops = 2 * slots * (width * 2 * units + groups * units * columns)
    return pl.pallas_call(
        functools.partial(layer_kernel, (n_attn, n_expert, n_hidden, n_pair, own, cap)),
        out_shape=jax.ShapeDtypeStruct(residual.shape, jnp.bfloat16),
        in_specs=[vmem] * 8 + [smem] + [hbm] * 2,
        out_specs=vmem,
        scratch_shapes=[
            pltpu.VMEM(gate_up_weight.shape[1:], jnp.bfloat16),
            pltpu.VMEM(down_weight.shape[1:], jnp.bfloat16),
            pltpu.VMEM(queries.shape[1:], jnp.bfloat16),
            pltpu.VMEM((n_hidden, n_attn * own, width), jnp.bfloat16),
            pltpu.VMEM((n_hidden, n_attn * own, width), jnp.bfloat16),
            pltpu.VMEM((n_attn, own, width), jnp.bfloat16),
            pltpu.VMEM((n_attn, own, width), jnp.bfloat16),
            pltpu.VMEM((own, width), jnp.float32),
            pltpu.VMEM((block, width), jnp.bfloat16),
            pltpu.VMEM((slots, width), jnp.bfloat16),
            pltpu.VMEM((groups, slots, units), jnp.bfloat16),
            pltpu.VMEM((slots, columns), jnp.bfloat16),
            pltpu.VMEM((n_attn, groups, block, columns), jnp.bfloat16),
            pltpu.SemaphoreType.DMA((2,)),
            pltpu.SemaphoreType.DMA((semaphores(n_attn, n_expert, n_hidden, n_pair),)),
            pltpu.SemaphoreType.DMA((semaphores(n_attn, n_expert, n_hidden, n_pair),)),
        ],
        compiler_params=pltpu.CompilerParams(
            collective_id=0, has_side_effects=True, vmem_limit_bytes=58 * 2**20
        ),
        cost_estimate=pl.CostEstimate(
            flops=flops,
            bytes_accessed=2 * (gate_up_weight.size + down_weight.size),
            transcendentals=slots * units,
        ),
    )(
        queries,
        keys,
        values,
        out_weight,
        residual,
        norm_gain[None],
        route_logits.transpose(0, 2, 1),
        expert_ids.transpose(0, 2, 1),
        doc_lengths,
        gate_up_weight,
        down_weight,
    )


def semaphores(n_attn, n_expert, n_hidden, n_pair):
    chunks = n_attn * n_pair
    return (
        4 * n_hidden
        + 4 * n_attn
        + n_expert
        + chunks
        + chunks * n_hidden
        + 2 * chunks * n_hidden
        + 2 * chunks * n_pair
        + 2 * chunks * n_hidden * n_pair
        + n_attn * n_expert * n_hidden * n_pair
    )


def capacity_of(own, n_expert):
    return max(2, (2 * own + n_expert - 1) // n_expert)


def body_of(mesh, *arrays):
    own = arrays[4].shape[1]
    cap = capacity_of(own, mesh.shape["expert"])
    whole_tiles = own % 16 == 0 and cap % 16 == 0
    if whole_tiles:
        return fused_body(mesh, *arrays)
    return plain_body(*arrays)


def solution(mesh):
    in_specs = (
        P(("expert", "pair"), None, ("attn", "hidden")),
        P(("expert", "pair"), None, "attn"),
        P(("expert", "pair"), None, "attn"),
        P(("attn", "hidden"), None),
        P(("expert", "pair"), ("attn", "hidden"), None),
        P(),
        P(("expert", "pair"), ("attn", "hidden"), None),
        P(("expert", "pair"), ("attn", "hidden"), None),
        P(("expert", "pair"), None),
        P("expert", None, None, ("attn", "hidden", "pair")),
        P("expert", "attn", ("hidden", "pair")),
    )
    out_specs = P(("expert", "pair"), ("attn", "hidden"), None)
    body = functools.partial(body_of, mesh)
    return jax.shard_map(body, mesh=mesh, in_specs=in_specs, out_specs=out_specs, check_vma=False)
```
